512 devices in a mesh: dp: 8 (over y), seq: 64 (over x, z, core).
Axes of the slice: x: 4, y: 8, z: 8, core: 2. Of those that a mesh axis runs over, the one named last changes fastest.
Arguments:
- inputs: bfloat16 [8, 8704, 6144], P('dp', 'seq'), may hold values from -6 to 6
- w_project: bfloat16 [6144, 3, 128], P(('dp', 'seq')), may hold values from -0.078125 to 0.078125
- w_output: bfloat16 [6144, 128], P(('dp', 'seq')), may hold values from -0.078125 to 0.078125
- norm_gain: float32 [128], replicated, may hold values from 0.1 to 1.9
- out_grad: bfloat16 [8, 8704, 6144], P('dp', 'seq'), may hold values from -6 to 6
Outputs:
- input_grad: bfloat16 [8, 8704, 6144], P('dp', 'seq')
The draws below stay inside these ranges and needn't reach their ends.
All inputs are finite; a program needn't handle non-finite values.
Results may differ from the reference program's by a relative error of at most 0.025.
Values may be sent and summed in bfloat16 or wider, within the bound.
No kernel may reach another device: no remote copies, remote signals or barrier semaphores. Data moves between devices by JAX's collectives and lax.ppermute only.
A program may use at most 64 MiB of HBM per device.

```python
import jax
import jax.numpy as jnp
from jax import lax

D = 6144
HEAD = 128
TOK_DEV = 136
LENGTH = 8704
BATCH = 8


def block_scale(own_key, extent, cuts, least, largest):
    factor_of, own = 1.0, jax.random.fold_in(own_key, 6)
    for dim, blocks in cuts:
        steps = jnp.exp(jax.random.uniform(jax.random.fold_in(own, dim), (blocks,), jnp.float32, least / len(cuts), largest / len(cuts)))
        factor_of = factor_of * jnp.repeat(steps, extent[dim] // blocks).reshape([-1 if axis == dim else 1 for axis in range(len(extent))])
    return factor_of


def centred(own_key, dims, scale, most, split=(), dtype=jnp.bfloat16):
    entries = jax.random.normal(own_key, dims, jnp.float32) * scale
    if len(split) > 0:
        entries = block_scale(own_key, dims, split, -0.22, 0.18) * entries
    return jnp.clip(entries, min=-most, max=most).astype(dtype)


def setup_inputs(seed: int = 0) -> dict:
    keys = jax.random.split(jax.random.key(seed), 6)
    return {
        "inputs": centred(keys[0], (BATCH, LENGTH, D), 1.0, 6.0, ((0, 8), (1, 64))),
        "w_project": centred(keys[1], (D, 3, HEAD), D ** -0.5, 0.078125, ((0, 512),)),
        "w_output": centred(keys[2], (D, HEAD), D ** -0.5, 0.078125, ((0, 512),)),
        "norm_gain": jnp.clip(1.0 + 0.18 * jax.random.normal(keys[3], (HEAD,), jnp.float32), 0.1, 1.9),
        "out_grad": centred(keys[4], (BATCH, LENGTH, D), 1.0, 6.0, ((0, 8), (1, 64))),
    }


def block_pass(tokens, grads_in, flat_proj, w_output, norm_gain):
    projected = jnp.dot(tokens, flat_proj, preferred_element_type=jnp.float32).astype(jnp.bfloat16)
    blocks = tokens.shape[0] // TOK_DEV
    queries = projected[:, :HEAD].reshape(blocks, TOK_DEV, HEAD).astype(jnp.float32)
    key_rows = projected[:, HEAD:2 * HEAD].reshape(blocks, TOK_DEV, HEAD).astype(jnp.float32)
    value_rows = projected[:, 2 * HEAD:].reshape(blocks, TOK_DEV, HEAD).astype(jnp.float32)
    causal = jnp.tril(jnp.ones((TOK_DEV, TOK_DEV), jnp.float32))
    scores = (jnp.einsum('btd,bsd->bts', queries, key_rows) * causal).astype(jnp.bfloat16).astype(jnp.float32)
    intra_part = jnp.einsum('bts,bsd->btd', scores, value_rows)
    local_state = jnp.einsum('bsk,bsv->bkv', key_rows, value_rows)
    prior_state = (jnp.cumsum(local_state, axis=0) - local_state).astype(jnp.bfloat16).astype(jnp.float32)
    attended = intra_part + jnp.einsum('btk,bkv->btv', queries, prior_state)
    inv_rms = lax.rsqrt(lax.optimization_barrier(jnp.mean(attended * attended, axis=-1, keepdims=True)) + 1e-06)
    head_grad = jnp.dot(grads_in, w_output, preferred_element_type=jnp.float32).reshape(blocks, TOK_DEV, HEAD)
    scaled = norm_gain * head_grad
    attn_grad = inv_rms * scaled - attended * inv_rms ** 3 * lax.optimization_barrier(jnp.mean(attended * scaled, axis=-1, keepdims=True))
    attn_grad = attn_grad.astype(jnp.bfloat16).astype(jnp.float32)
    prob_grad = (jnp.einsum('btv,bsv->bts', attn_grad, value_rows) * causal).astype(jnp.bfloat16).astype(jnp.float32)
    local_grad = jnp.einsum('btk,btv->bkv', queries, attn_grad)
    later_state = (jnp.flip(jnp.cumsum(jnp.flip(local_grad, 0), axis=0), 0) - local_grad).astype(jnp.bfloat16).astype(jnp.float32)
    query_grad = jnp.einsum('bts,bsk->btk', prob_grad, key_rows) + jnp.einsum('btv,bkv->btk', attn_grad, prior_state)
    key_grad = jnp.einsum('bts,btk->bsk', prob_grad, queries) + jnp.einsum('bsv,bkv->bsk', value_rows, later_state)
    value_grad = jnp.einsum('bts,btv->bsv', scores, attn_grad) + jnp.einsum('bsk,bkv->bsv', key_rows, later_state)
    joined = jnp.concatenate([query_grad, key_grad, value_grad], axis=-1).astype(jnp.bfloat16)
    joined = joined.reshape(tokens.shape[0], 3 * HEAD)
    result = lax.dot_general(joined, flat_proj, (((1,), (1,)), ((), ())), preferred_element_type=jnp.float32)
    return result.astype(jnp.bfloat16)

def reference(inputs, w_project, w_output, norm_gain, out_grad):
    flat_proj = w_project.reshape(D, 3 * HEAD)

    def one_sequence(pair):
        return block_pass(pair[0], pair[1], flat_proj, w_output, norm_gain)
    return lax.map(one_sequence, (inputs, out_grad))
```

```python
import jax
import jax.numpy as jnp
from jax import lax
from jax.sharding import Mesh
from jax.sharding import PartitionSpec as P

SEQ = ("x", "z", "core")
DP_SEQ = ("dp", "x", "z", "core")
ROWS = ("dp", "z")


def contract(left, right, left_dim, right_dim):
    return lax.dot_general(
        left, right, (((left_dim,), (right_dim,)), ((), ())), preferred_element_type=jnp.float32
    )


def spread(block, axes):
    peers = lax.axis_size(axes)
    return lax.all_to_all(
        jnp.broadcast_to(block[None], (peers, *block.shape)), axes, 0, 0, tiled=True
    )


def core_swap(block):
    return lax.ppermute(block, "core", [(0, 1), (1, 0)])


def by_core(mine, other):
    first = lax.axis_index("core") == 0
    return jnp.where(first, mine, other), jnp.where(first, other, mine)


def rows_in_order(block):
    xs, dps = lax.axis_size("x"), lax.axis_size("dp")
    head = block.shape[-1]
    return block.reshape(xs, dps, -1, head).swapaxes(0, 1).reshape(-1, head)


def other_blocks(local, reverse):
    head = local.shape[0]
    peers = lax.axis_size(SEQ)
    pieces = local.astype(jnp.bfloat16).reshape(peers, head // peers, head)
    pieces = lax.all_to_all(pieces, SEQ, 0, 0, tiled=True).reshape(peers, -1)
    to = lax.broadcasted_iota(jnp.int32, (peers, peers), 0)
    frm = lax.broadcasted_iota(jnp.int32, (peers, peers), 1)
    mask = ((frm > to) if reverse else (frm < to)).astype(jnp.bfloat16)
    sums = contract(mask, pieces, 1, 0).astype(jnp.bfloat16)
    sums = lax.all_to_all(sums.reshape(peers, head // peers, head), SEQ, 0, 0, tiled=True)
    return sums.reshape(head, head)


def per_device(inputs, w_project, w_output, norm_gain, out_grad):
    tokens = inputs[0]
    grads_in = out_grad[0]
    count = tokens.shape[0]
    bf16 = jnp.bfloat16

    to_first = jnp.concatenate([w_project[:, 1], w_project[:, 0]], axis=1)
    to_second = jnp.concatenate([w_project[:, 2], w_output], axis=1)
    pair = lax.all_to_all(jnp.stack([to_first, to_second]), "core", 0, 0, tiled=True)
    head = w_output.shape[1]
    pair = pair.reshape(-1, 2 * head)

    def gathered(block):
        plane = spread(block, ROWS).reshape(-1, head)
        return spread(plane, "x")

    kv_mine = gathered(pair[:, :head])
    qo_mine = gathered(pair[:, head:])
    w_key, w_value = by_core(kv_mine, core_swap(kv_mine))
    w_query, w_out = by_core(qo_mine, core_swap(qo_mine))
    w_query, w_key, w_value, w_out = map(rows_in_order, (w_query, w_key, w_value, w_out))

    key_rows = contract(tokens, w_key, 1, 0).astype(bf16)
    value_rows = contract(tokens, w_value, 1, 0).astype(bf16)
    local_state = contract(key_rows, value_rows, 0, 0)
    prior_state = other_blocks(local_state, False)

    queries = contract(tokens, w_query, 1, 0).astype(bf16)
    head_grad = contract(grads_in, w_out, 1, 0)
    row_ids = lax.broadcasted_iota(jnp.int32, (count, count), 0)
    col_ids = lax.broadcasted_iota(jnp.int32, (count, count), 1)
    causal = row_ids >= col_ids
    scores = jnp.where(causal, contract(queries, key_rows, 1, 1), 0.0).astype(bf16)
    attended = contract(scores, value_rows, 1, 0) + contract(queries, prior_state, 1, 0)
    inv_rms = lax.rsqrt(jnp.mean(attended * attended, axis=-1, keepdims=True) + 1e-06)
    scaled = norm_gain * head_grad
    attn_grad = inv_rms * scaled - attended * inv_rms**3 * jnp.mean(
        attended * scaled, axis=-1, keepdims=True
    )
    attn_grad = attn_grad.astype(bf16)
    local_grad = contract(queries, attn_grad, 0, 0)
    later_state = other_blocks(local_grad, True)
    prob_grad = jnp.where(causal, contract(attn_grad, value_rows, 1, 1), 0.0).astype(bf16)
    query_grad = contract(prob_grad, key_rows, 1, 0) + contract(attn_grad, prior_state, 1, 1)
    key_grad = contract(prob_grad, queries, 0, 0) + contract(value_rows, later_state, 1, 1)
    value_grad = contract(scores, attn_grad, 0, 0) + contract(key_rows, later_state, 1, 0)
    result = (
        contract(query_grad.astype(bf16), w_query, 1, 1)
        + contract(key_grad.astype(bf16), w_key, 1, 1)
        + contract(value_grad.astype(bf16), w_value, 1, 1)
    )
    return result.astype(bf16)[None]


def solution(mesh):
    split = Mesh(mesh.devices.reshape(mesh.shape["dp"], 4, 8, 2), DP_SEQ)
    in_specs = (P("dp", SEQ, None), P(DP_SEQ, None, None), P(DP_SEQ, None), P(), P("dp", SEQ, None))
    out_specs = P("dp", SEQ, None)
    return jax.shard_map(
        per_device, mesh=split, in_specs=in_specs, out_specs=out_specs, check_vma=False
    )
```

```python
import functools

import jax
import jax.numpy as jnp
from jax import lax
from jax.experimental import pallas as pl
from jax.experimental.pallas import tpu as pltpu
from jax.sharding import Mesh
from jax.sharding import PartitionSpec as P

SEQ = ("x", "z", "core")
DP_SEQ = ("dp", "x", "z", "core")
ROWS = ("dp", "z")
BF16 = jnp.bfloat16
F32 = jnp.float32
LIMIT = 40 * 1024 * 1024
SMEM = pl.BlockSpec(memory_space=pltpu.SMEM)
VMEM = pl.BlockSpec(memory_space=pltpu.VMEM)


def contract(left, right, left_dim, right_dim):
    return lax.dot_general(
        left, right, (((left_dim,), (right_dim,)), ((), ())), preferred_element_type=F32
    )


def cost(flops, moved):
    return pl.CostEstimate(flops=flops, bytes_accessed=moved, transcendentals=0)


def spread(block, axes):
    peers = lax.axis_size(axes)
    return lax.all_to_all(
        jnp.broadcast_to(block[None], (peers, *block.shape)), axes, 0, 0, tiled=True
    )


def after(value, *events):
    return lax.optimization_barrier((value, *events))[0]


def core_swap(block):
    return lax.ppermute(block, "core", [(0, 1), (1, 0)])


def columns_kernel(parts, place_ref, tokens_ref, *out_refs):
    width = tokens_ref.shape[1] // parts
    count = tokens_ref.shape[0]
    low = lax.broadcasted_iota(jnp.int32, (count, 128), 1) < 64
    for to in range(4):
        step = lax.rem(to - place_ref[0] + 4, 4)
        first = to * 192
        whole_at = first if to % 2 == 0 else first + 64
        half_at = (first + 128 if to % 2 == 0 else first) // 128 * 128

        pairs = []
        for p in range(parts // 2):
            even = tokens_ref[:, 2 * p * width + half_at : 2 * p * width + half_at + 128]
            odd = tokens_ref[:, (2 * p + 1) * width + half_at : (2 * p + 1) * width + half_at + 128]
            even, odd = even.astype(F32), odd.astype(F32)
            if to % 2 == 0:
                odd = pltpu.roll(odd, 64, 1)
            else:
                even = pltpu.roll(even, 64, 1)
            pairs.append(jnp.where(low, even, odd).astype(BF16))
        for k in range(4):

            @pl.when(step == k)
            def _(k=k, whole_at=whole_at, pairs=pairs):
                for p in range(parts):
                    out_refs[k][:, p * 128 : (p + 1) * 128] = tokens_ref[
                        :, p * width + whole_at : p * width + whole_at + 128
                    ]
                for p, pair in enumerate(pairs):
                    at = parts * 128 + p * 128
                    out_refs[k][:, at : at + 128] = pair


def split_columns(place, tokens, parts):
    count, depth = tokens.shape
    return pl.pallas_call(
        functools.partial(columns_kernel, parts),
        out_shape=[jax.ShapeDtypeStruct((count, depth // 4), BF16)] * 4,
        in_specs=[SMEM, VMEM],
        out_specs=[VMEM] * 4,
        compiler_params=pltpu.CompilerParams(vmem_limit_bytes=LIMIT),
        cost_estimate=cost(0, 4 * tokens.size),
    )(place, tokens)


def partial_kernel(parts, place_ref, t0, t1, t2, t3, mine_ref, other_ref, out_ref, held):
    rows = mine_ref.shape[0] // parts
    odd = lax.rem(place_ref[0], 2)
    whole_at, half_at = odd * 64, (1 - odd) * 128
    for p in range(parts):
        for n, ref in enumerate((mine_ref, other_ref)):
            columns = slice(n * 128, (n + 1) * 128)
            held[p * 128 : (p + 1) * 128, columns] = ref[
                pl.ds(pl.multiple_of(p * rows + whole_at, 64), 128), :
            ]
            at = parts * 128 + p * 64
            held[at : at + 64, columns] = ref[
                pl.ds(pl.multiple_of(p * rows + half_at, 64), 64), :
            ]
    for k, ref in enumerate((t0, t1, t2, t3)):
        source = lax.rem(place_ref[0] - k + 4, 4)
        out_ref[source] = contract(ref[...], held[...], 1, 0).astype(BF16)


def partial_sums(place, pieces, mine, other, parts):
    count, depth = pieces[0].shape
    return pl.pallas_call(
        functools.partial(partial_kernel, parts),
        out_shape=jax.ShapeDtypeStruct((4, count, 256), BF16),
        in_specs=[SMEM] + [VMEM] * 6,
        out_specs=VMEM,
        scratch_shapes=[pltpu.VMEM((depth, 256), BF16)],
        compiler_params=pltpu.CompilerParams(vmem_limit_bytes=LIMIT),
        cost_estimate=cost(8 * count * depth * 256, 8 * count * depth + 4 * depth * 128),
    )(place, *pieces, mine, other)


def state_kernel(place_ref, parts_ref, key_ref, value_ref, state_ref):
    total = parts_ref[0].astype(F32)
    for k in range(1, 4):
        total += parts_ref[k].astype(F32)
    total = total.astype(BF16)
    mine, other = total[:, :128], total[:, 128:]
    first = place_ref[1] == 0
    keys = jnp.where(first, mine, other)
    values = jnp.where(first, other, mine)
    key_ref[...] = keys
    value_ref[...] = values
    state_ref[...] = contract(keys, values, 0, 0).astype(BF16)


def keys_values_state(place, parts):
    count = parts.shape[1]
    row = jax.ShapeDtypeStruct((count, 128), BF16)
    return pl.pallas_call(
        state_kernel,
        out_shape=[row, row, jax.ShapeDtypeStruct((128, 128), BF16)],
        in_specs=[SMEM, VMEM],
        out_specs=[VMEM] * 3,
        compiler_params=pltpu.CompilerParams(vmem_limit_bytes=LIMIT),
        cost_estimate=cost(2 * count * 128 * 128, 2 * parts.size),
    )(place, parts)


def query_kernel(steps, place_ref, tokens_ref, grads_ref, mine_ref, other_ref, q_ref, hg_ref, qs, hs):
    step = pl.program_id(0)

    @pl.when(step == 0)
    def _():
        qs[...] = jnp.zeros_like(qs)
        hs[...] = jnp.zeros_like(hs)

    mine = mine_ref[...].reshape(-1, 128)
    other = other_ref[...].reshape(-1, 128)
    first = place_ref[1] == 0
    w_query = jnp.where(first, mine, other)
    w_out = jnp.where(first, other, mine)
    qs[...] += contract(tokens_ref[...], w_query, 1, 0)
    hs[...] += contract(grads_ref[...], w_out, 1, 0)

    @pl.when(step == steps - 1)
    def _():
        q_ref[...] = qs[...].astype(BF16)
        hg_ref[...] = hs[...]


def queries_head_grad(place, tokens, grads_in, mine, other):
    count, depth = tokens.shape
    xs, steps, rows, _ = mine.shape
    wide = pl.BlockSpec((count, depth // steps), lambda i: (0, i))
    weight = pl.BlockSpec((xs, 1, rows, 128), lambda i: (0, i, 0, 0))
    whole = pl.BlockSpec((count, 128), lambda i: (0, 0))
    return pl.pallas_call(
        functools.partial(query_kernel, steps),
        grid=(steps,),
        out_shape=[
            jax.ShapeDtypeStruct((count, 128), BF16),
            jax.ShapeDtypeStruct((count, 128), F32),
        ],
        in_specs=[SMEM, wide, wide, weight, weight],
        out_specs=[whole, whole],
        scratch_shapes=[pltpu.VMEM((count, 128), F32)] * 2,
        compiler_params=pltpu.CompilerParams(vmem_limit_bytes=LIMIT),
        cost_estimate=cost(4 * count * depth * 128, 4 * (tokens.size + mine.size)),
    )(place, tokens, grads_in, mine, other)


def causal_of(count):
    rows = lax.broadcasted_iota(jnp.int32, (count, count), 0)
    return rows >= lax.broadcasted_iota(jnp.int32, (count, count), 1)


def scores_kernel(q_ref, k_ref, v_ref, scores_ref, intra_ref):
    scores = contract(q_ref[...], k_ref[...], 1, 1)
    scores = jnp.where(causal_of(scores.shape[0]), scores, 0.0).astype(BF16)
    scores_ref[...] = scores
    intra_ref[...] = contract(scores, v_ref[...], 1, 0)


def inner_scores(queries, keys, values):
    count = queries.shape[0]
    return pl.pallas_call(
        scores_kernel,
        out_shape=[
            jax.ShapeDtypeStruct((count, count), BF16),
            jax.ShapeDtypeStruct((count, 128), F32),
        ],
        in_specs=[VMEM] * 3,
        out_specs=[VMEM] * 2,
        compiler_params=pltpu.CompilerParams(vmem_limit_bytes=LIMIT),
        cost_estimate=cost(4 * count * count * 128, 8 * count * 128),
    )(queries, keys, values)


def grad_kernel(q_ref, intra_ref, prior_ref, hg_ref, gain_ref, attn_ref, state_ref):
    queries = q_ref[...]
    attended = intra_ref[...] + contract(queries, prior_ref[...], 1, 0)
    inv_rms = lax.rsqrt(jnp.mean(attended * attended, axis=-1, keepdims=True) + 1e-06)
    scaled = gain_ref[...] * hg_ref[...]
    mean = jnp.mean(attended * scaled, axis=-1, keepdims=True)
    attn_grad = inv_rms * scaled - attended * (inv_rms * inv_rms * inv_rms) * mean
    attn_grad = attn_grad.astype(BF16)
    attn_ref[...] = attn_grad
    state_ref[...] = contract(queries, attn_grad, 0, 0).astype(BF16)


def attention_grad(queries, intra, prior, head_grad, gain):
    count = queries.shape[0]
    return pl.pallas_call(
        grad_kernel,
        out_shape=[
            jax.ShapeDtypeStruct((count, 128), BF16),
            jax.ShapeDtypeStruct((128, 128), BF16),
        ],
        in_specs=[VMEM] * 5,
        out_specs=[VMEM] * 2,
        compiler_params=pltpu.CompilerParams(vmem_limit_bytes=LIMIT),
        cost_estimate=cost(4 * count * 128 * 128, 16 * count * 128),
    )(queries, intra, prior, head_grad, gain)


def inner_kernel(q_ref, k_ref, v_ref, scores_ref, attn_ref, prior_ref, dq_ref, dk_ref, dv_ref):
    attn_grad = attn_ref[...]
    prob = contract(attn_grad, v_ref[...], 1, 1)
    prob = jnp.where(causal_of(prob.shape[0]), prob, 0.0).astype(BF16)
    dq_ref[...] = contract(prob, k_ref[...], 1, 0) + contract(attn_grad, prior_ref[...], 1, 1)
    dk_ref[...] = contract(prob, q_ref[...], 0, 0)
    dv_ref[...] = contract(scores_ref[...], attn_grad, 0, 0)


def inner_grads(queries, keys, values, scores, attn_grad, prior):
    count = queries.shape[0]
    row = jax.ShapeDtypeStruct((count, 128), F32)
    return pl.pallas_call(
        inner_kernel,
        out_shape=[row] * 3,
        in_specs=[VMEM] * 6,
        out_specs=[VMEM] * 3,
        compiler_params=pltpu.CompilerParams(vmem_limit_bytes=LIMIT),
        cost_estimate=cost(10 * count * count * 128, 20 * count * 128),
    )(queries, keys, values, scores, attn_grad, prior)


def output_kernel(
    place_ref, dq, dk, dv, k_ref, v_ref, later, q0, q1, kv_mine, kv_other, out_ref, joined
):
    first = place_ref[1] == 0

    @pl.when(pl.program_id(0) == 0)
    def _():
        key_grad = (dk[...] + contract(v_ref[...], later[...], 1, 1)).astype(BF16)
        value_grad = (dv[...] + contract(k_ref[...], later[...], 1, 0)).astype(BF16)
        joined[0] = dq[...].astype(BF16)
        joined[1] = jnp.where(first, key_grad, value_grad)
        joined[2] = jnp.where(first, value_grad, key_grad)

    w_query = jnp.where(first, q0[...].reshape(-1, 128), q1[...].reshape(-1, 128))
    total = contract(joined[0], w_query, 1, 1)
    total += contract(joined[1], kv_mine[...].reshape(-1, 128), 1, 1)
    total += contract(joined[2], kv_other[...].reshape(-1, 128), 1, 1)
    out_ref[...] = total.astype(BF16)


def output(place, dq, dk, dv, keys, values, later, qo_mine, qo_other, kv_mine, kv_other):
    count = dq.shape[0]
    xs, steps, rows, _ = qo_mine.shape
    depth = xs * steps * rows
    weight = pl.BlockSpec((xs, 1, rows, 128), lambda i, s: (0, i, 0, 0))
    on_first = pl.BlockSpec((xs, 1, rows, 128), lambda i, s: (0, i * (1 - s[1]), 0, 0))
    on_second = pl.BlockSpec((xs, 1, rows, 128), lambda i, s: (0, i * s[1], 0, 0))
    row = pl.BlockSpec((count, 128), lambda i, s: (0, 0))
    square = pl.BlockSpec((128, 128), lambda i, s: (0, 0))
    return pl.pallas_call(
        output_kernel,
        out_shape=jax.ShapeDtypeStruct((count, depth), BF16),
        grid_spec=pltpu.PrefetchScalarGridSpec(
            num_scalar_prefetch=1,
            grid=(steps,),
            in_specs=[row] * 5 + [square, on_first, on_second, weight, weight],
            out_specs=pl.BlockSpec((count, depth // steps), lambda i, s: (0, i)),
            scratch_shapes=[pltpu.VMEM((3, count, 128), BF16)],
        ),
        compiler_params=pltpu.CompilerParams(vmem_limit_bytes=LIMIT),
        cost_estimate=cost(6 * count * depth * 128, 2 * (3 * depth * 128 + count * depth)),
    )(place, dq, dk, dv, keys, values, later, qo_mine, qo_other, kv_mine, kv_other)


def deal(local):
    head = local.shape[0]
    peers = lax.axis_size(SEQ)
    pieces = local.reshape(peers, head // peers, head)
    return lax.all_to_all(pieces, SEQ, 0, 0, tiled=True)


def other_blocks(pieces, reverse):
    peers, _, head = pieces.shape
    pieces = pieces.reshape(peers, -1)
    to = lax.broadcasted_iota(jnp.int32, (peers, peers), 0)
    frm = lax.broadcasted_iota(jnp.int32, (peers, peers), 1)
    mask = ((frm > to) if reverse else (frm < to)).astype(BF16)
    sums = contract(mask, pieces, 1, 0).astype(BF16)
    sums = lax.all_to_all(sums.reshape(peers, head // peers, head), SEQ, 0, 0, tiled=True)
    return sums.reshape(head, head)


def per_device(inputs, w_project, w_output, norm_gain, out_grad):
    tokens = inputs[0]
    grads_in = out_grad[0]
    head = w_output.shape[1]
    dps, xs = lax.axis_size("dp"), lax.axis_size("x")
    place = jnp.stack([lax.axis_index("x"), lax.axis_index("core")]).astype(jnp.int32)

    to_first = jnp.concatenate([w_project[:, 1], w_project[:, 0]], axis=1)
    to_second = jnp.concatenate([w_project[:, 2], w_output], axis=1)
    pair = lax.all_to_all(jnp.stack([to_first, to_second]), "core", 0, 0, tiled=True)
    plane = spread(pair.reshape(-1, 2 * head), ROWS).reshape(-1, 2 * head)
    kv_plane, qo_plane = plane[:, :head], plane[:, head:]

    pieces = split_columns(place, tokens, dps)
    moved = [pieces[0]]
    for k in range(1, xs):
        moved.append(lax.ppermute(pieces[k], "x", [(i, (i + k) % xs) for i in range(xs)]))
    kv_near = after(kv_plane, pieces[0])
    kv_far = core_swap(kv_near)
    sums = partial_sums(place, moved, kv_near, kv_far, dps)
    qo_plane = after(qo_plane, sums)
    sums = lax.all_to_all(sums, "x", 0, 0, tiled=True)
    keys, values, local_state = keys_values_state(place, sums)
    state_pieces = deal(local_state)
    kv_plane = after(kv_plane, state_pieces)
    prior_state = other_blocks(state_pieces, False)

    def whole(block):
        return lax.all_gather(block, "x").reshape(xs, dps, -1, head)

    qo_mine = after(whole(qo_plane), state_pieces)
    qo_other = core_swap(qo_mine)

    queries, head_grad = queries_head_grad(place, tokens, grads_in, qo_mine, qo_other)
    scores, intra = inner_scores(queries, keys, values)
    attn_grad, local_grad = attention_grad(
        queries, intra, prior_state, head_grad, norm_gain.reshape(1, head)
    )
    grad_pieces = deal(local_grad)
    kv_mine = after(whole(kv_plane), grad_pieces)
    kv_other = core_swap(kv_mine)
    later_state = other_blocks(grad_pieces, True)
    grads = inner_grads(queries, keys, values, scores, attn_grad, prior_state)
    result = output(
        place, *grads, keys, values, later_state, qo_mine, qo_other, kv_mine, kv_other
    )
    return result[None]


def solution(mesh):
    split = Mesh(mesh.devices.reshape(mesh.shape["dp"], 4, 8, 2), DP_SEQ)
    in_specs = (P("dp", SEQ, None), P(DP_SEQ, None, None), P(DP_SEQ, None), P(), P("dp", SEQ, None))
    out_specs = P("dp", SEQ, None)
    return jax.shard_map(
        per_device, mesh=split, in_specs=in_specs, out_specs=out_specs, check_vma=False
    )
```

```python
import functools

import jax
import jax.numpy as jnp
from jax import lax
from jax.experimental import pallas as pl
from jax.experimental.pallas import tpu as pltpu
from jax.sharding import Mesh
from jax.sharding import PartitionSpec as P

SEQ = ("x", "z", "core")
DP_SEQ = ("dp", "x", "z", "core")
ROWS = ("dp", "z")
BF16 = jnp.bfloat16
F32 = jnp.float32
LIMIT = 16 * 1024 * 1024
LONG = 30_000_000_000
SMEM = pl.BlockSpec(memory_space=pltpu.SMEM)
VMEM = pl.BlockSpec(memory_space=pltpu.VMEM)


def contract(left, right, left_dim, right_dim):
    return lax.dot_general(
        left, right, (((left_dim,), (right_dim,)), ((), ())), preferred_element_type=F32
    )


def cost(flops, moved):
    return pl.CostEstimate(flops=flops, bytes_accessed=moved, transcendentals=0)


def after(value, *events):
    return lax.optimization_barrier((value, *events))[0]


def core_swap(block):
    return lax.ppermute(block, "core", [(0, 1), (1, 0)])


def put_rows(parts, place_ref, blocks, out_ref):
    rows = blocks[0].shape[0] // parts
    for k, ref in enumerate(blocks):
        source = lax.rem(place_ref[0] - k + 4, 4)
        for p in range(parts):
            at = pl.multiple_of((p * 4 + source) * rows, 64)
            out_ref[pl.ds(at, rows), :] = ref[p * rows : (p + 1) * rows, :]


def project_kernel(parts, place_ref, *refs):
    tokens, blocks, (weight_ref, own_ref, send_ref) = refs[:-7], refs[-7:-3], refs[-3:]
    put_rows(parts, place_ref, blocks, weight_ref)

    def products(own, far):
        own_ref[...] = contract(own[...], weight_ref[...], 1, 0).astype(own_ref.dtype)
        send_ref[...] = contract(far[...], weight_ref[...], 1, 0).astype(send_ref.dtype)

    if len(tokens) == 2:
        products(*tokens)
    else:
        pl.when(place_ref[1] == 0)(lambda: products(*tokens[:2]))
        pl.when(place_ref[1] != 0)(lambda: products(*tokens[2:]))


def project(place, tokens, blocks, parts, dtype):
    count, depth = tokens[0].shape
    row = jax.ShapeDtypeStruct((count, 128), dtype)
    return pl.pallas_call(
        functools.partial(project_kernel, parts),
        out_shape=[jax.ShapeDtypeStruct((depth, 128), BF16), row, row],
        in_specs=[SMEM] + [VMEM] * (len(tokens) + 4),
        out_specs=[VMEM] * 3,
        compiler_params=pltpu.CompilerParams(vmem_limit_bytes=LIMIT),
        cost_estimate=cost(LONG, 4 * count * depth + 4 * depth * 128),
    )(place, *tokens, *blocks)


def state_kernel(place_ref, own_ref, recv_ref, key_ref, value_ref, state_ref):
    own, recv = own_ref[...], recv_ref[...]
    first = place_ref[1] == 0
    keys, values = jnp.where(first, own, recv), jnp.where(first, recv, own)
    key_ref[...] = keys
    value_ref[...] = values
    state_ref[...] = contract(keys, values, 0, 0).astype(BF16)


def keys_values_state(place, own, recv):
    row = jax.ShapeDtypeStruct(own.shape, BF16)
    return pl.pallas_call(
        state_kernel,
        out_shape=[row, row, jax.ShapeDtypeStruct((128, 128), BF16)],
        in_specs=[SMEM] + [VMEM] * 2,
        out_specs=[VMEM] * 3,
        compiler_params=pltpu.CompilerParams(vmem_limit_bytes=LIMIT),
        cost_estimate=cost(2 * own.size * 128, 8 * own.size),
    )(place, own, recv)


def gate_kernel(in_ref, out_ref):
    out_ref[...] = in_ref[...]


def gate(value):
    return pl.pallas_call(
        gate_kernel,
        out_shape=jax.ShapeDtypeStruct(value.shape, value.dtype),
        in_specs=[VMEM],
        out_specs=VMEM,
        compiler_params=pltpu.CompilerParams(vmem_limit_bytes=LIMIT),
        cost_estimate=cost(LONG, 4 * value.size),
    )(value)


def causal_of(count):
    rows = lax.broadcasted_iota(jnp.int32, (count, count), 0)
    return rows >= lax.broadcasted_iota(jnp.int32, (count, count), 1)


def grad_kernel(
    place_ref, near_ref, far_ref, k_ref, v_ref, prior_ref, gain_ref,
    q_ref, scores_ref, attn_ref, state_ref,
):
    first = place_ref[1] == 0
    near, far = near_ref[...], far_ref[...]
    queries = jnp.where(first, near, far).astype(BF16)
    head_grad = jnp.where(first, far, near)
    q_ref[...] = queries
    scores = contract(queries, k_ref[...], 1, 1)
    scores = jnp.where(causal_of(scores.shape[0]), scores, 0.0).astype(BF16)
    scores_ref[...] = scores
    attended = contract(scores, v_ref[...], 1, 0) + contract(queries, prior_ref[...], 1, 0)
    inv_rms = lax.rsqrt(jnp.mean(attended * attended, axis=-1, keepdims=True) + 1e-06)
    scaled = gain_ref[...] * head_grad
    mean = jnp.mean(attended * scaled, axis=-1, keepdims=True)
    attn_grad = inv_rms * scaled - attended * (inv_rms * inv_rms * inv_rms) * mean
    attn_grad = attn_grad.astype(BF16)
    attn_ref[...] = attn_grad
    state_ref[...] = contract(queries, attn_grad, 0, 0).astype(BF16)


def attention_grad(place, near, far, keys, values, prior, gain):
    count = keys.shape[0]
    row = jax.ShapeDtypeStruct((count, 128), BF16)
    return pl.pallas_call(
        grad_kernel,
        out_shape=[
            row,
            jax.ShapeDtypeStruct((count, count), BF16),
            row,
            jax.ShapeDtypeStruct((128, 128), BF16),
        ],
        in_specs=[SMEM] + [VMEM] * 6,
        out_specs=[VMEM] * 4,
        compiler_params=pltpu.CompilerParams(vmem_limit_bytes=LIMIT),
        cost_estimate=cost(LONG, 16 * count * 128),
    )(place, near, far, keys, values, prior, gain)


def inner_kernel(
    place_ref, q_ref, k_ref, v_ref, scores_ref, attn_ref, prior_ref, near_ref, far_ref,
    base_ref, dk_ref, dv_ref, dq,
):
    @pl.when(pl.program_id(0) == 0)
    def _():
        attn_grad = attn_ref[...]
        prob = contract(attn_grad, v_ref[...], 1, 1)
        prob = jnp.where(causal_of(prob.shape[0]), prob, 0.0).astype(BF16)
        query_grad = contract(prob, k_ref[...], 1, 0) + contract(attn_grad, prior_ref[...], 1, 1)
        dq[...] = query_grad.astype(BF16)
        dk_ref[...] = contract(prob, q_ref[...], 0, 0)
        dv_ref[...] = contract(scores_ref[...], attn_grad, 0, 0)

    weight = jnp.where(place_ref[1] == 0, near_ref[...], far_ref[...])
    base_ref[...] = contract(dq[...], weight, 1, 1)


def inner_grads(place, queries, keys, values, scores, attn_grad, prior, near, far):
    count, depth, steps = queries.shape[0], near.shape[0], 4
    row = pl.BlockSpec((count, 128), lambda i: (0, 0))
    square = pl.BlockSpec((128, 128), lambda i: (0, 0))
    inner = pl.BlockSpec((count, count), lambda i: (0, 0))
    weight = pl.BlockSpec((depth // steps, 128), lambda i: (i, 0))
    return pl.pallas_call(
        inner_kernel,
        grid=(steps,),
        out_shape=[
            jax.ShapeDtypeStruct((count, depth), F32),
            jax.ShapeDtypeStruct((count, 128), F32),
            jax.ShapeDtypeStruct((count, 128), F32),
        ],
        in_specs=[SMEM, row, row, row, inner, row, square, weight, weight],
        out_specs=[pl.BlockSpec((count, depth // steps), lambda i: (0, i)), row, row],
        scratch_shapes=[pltpu.VMEM((count, 128), BF16)],
        compiler_params=pltpu.CompilerParams(vmem_limit_bytes=LIMIT),
        cost_estimate=cost(2 * count * depth * 128, 4 * count * depth + 4 * depth * 128),
    )(place, queries, keys, values, scores, attn_grad, prior, near, far)


def output_kernel(place_ref, base, dk, dv, k_ref, v_ref, later, near_ref, far_ref, out_ref, joined):
    @pl.when(pl.program_id(0) == 0)
    def _():
        first = place_ref[1] == 0
        key_grad = (dk[...] + contract(v_ref[...], later[...], 1, 1)).astype(BF16)
        value_grad = (dv[...] + contract(k_ref[...], later[...], 1, 0)).astype(BF16)
        joined[:, :128] = jnp.where(first, key_grad, value_grad)
        joined[:, 128:] = jnp.where(first, value_grad, key_grad)

    weight = jnp.concatenate([near_ref[...], far_ref[...]], axis=1)
    total = base[...] + contract(joined[...], weight, 1, 1)
    out_ref[...] = total.astype(BF16)


def output(place, base, dk, dv, keys, values, later, near, far):
    count, depth = base.shape
    steps = 4
    row = pl.BlockSpec((count, 128), lambda i: (0, 0))
    square = pl.BlockSpec((128, 128), lambda i: (0, 0))
    wide = pl.BlockSpec((count, depth // steps), lambda i: (0, i))
    weight = pl.BlockSpec((depth // steps, 128), lambda i: (i, 0))
    return pl.pallas_call(
        output_kernel,
        grid=(steps,),
        out_shape=jax.ShapeDtypeStruct((count, depth), BF16),
        in_specs=[SMEM, wide, row, row, row, row, square, weight, weight],
        out_specs=wide,
        scratch_shapes=[pltpu.VMEM((count, 256), BF16)],
        compiler_params=pltpu.CompilerParams(vmem_limit_bytes=LIMIT),
        cost_estimate=cost(4 * count * depth * 128, 4 * depth * 128 + 6 * count * depth),
    )(place, base, dk, dv, keys, values, later, near, far)


def sums_kernel(reverse, in_ref, out_ref):
    each = in_ref.shape[0] // 64
    to = lax.broadcasted_iota(jnp.int32, (128, 128), 0)
    frm = lax.broadcasted_iota(jnp.int32, (128, 128), 1)
    others = (frm // each > to // each) if reverse else (frm // each < to // each)
    mask = jnp.where(others & (frm % each == to % each), 1.0, 0.0).astype(BF16)
    out_ref[...] = contract(mask, in_ref[...], 1, 0).astype(BF16)


def sums_of(pieces, reverse):
    return pl.pallas_call(
        functools.partial(sums_kernel, reverse),
        out_shape=jax.ShapeDtypeStruct(pieces.shape, BF16),
        in_specs=[VMEM],
        out_specs=VMEM,
        compiler_params=pltpu.CompilerParams(vmem_limit_bytes=LIMIT),
        cost_estimate=cost(LONG, 4 * pieces.size),
    )(pieces)


def exchange(state):
    peers, head = lax.axis_size(SEQ), state.shape[1]
    pieces = state.reshape(peers, -1, head)
    return lax.all_to_all(pieces, SEQ, 0, 0, tiled=True).reshape(state.shape)


def per_device(inputs, w_project, w_output, norm_gain, out_grad):
    tokens = inputs[0]
    grads_in = out_grad[0]
    head = w_output.shape[1]
    dps, zs, xs = lax.axis_size("dp"), lax.axis_size("z"), lax.axis_size("x")
    place = jnp.stack([lax.axis_index("x"), lax.axis_index("core")]).astype(jnp.int32)
    on_first = lax.axis_index("core") == 0

    rows = jnp.concatenate([w_project.reshape(-1, 3 * head), w_output], axis=1)
    rows = lax.all_gather(rows, "core", axis=0, tiled=True)
    kv_rows = jnp.where(on_first, rows[:, head : 2 * head], rows[:, 2 * head : 3 * head])
    qo_rows = jnp.where(on_first, rows[:, :head], rows[:, 3 * head :])

    def over_planes(block):
        copies = jnp.broadcast_to(block[None], (dps * zs, *block.shape))
        return lax.all_to_all(copies, ROWS, 0, 0, tiled=True).reshape(-1, head)

    def over_x(block):
        shifts = {k: lax.ppermute(block, "x", [(i, (i + k) % xs) for i in range(xs)]) for k in (2, 1, 3)}
        return [block, shifts[1], shifts[2], shifts[3]]

    tokens_far, grads_far = core_swap(tokens), core_swap(grads_in)
    kv_plane = over_planes(kv_rows)
    qo_plane = over_planes(after(qo_rows, kv_plane))
    kv_near, own, send = project(place, (tokens, tokens_far), over_x(kv_plane), dps, BF16)
    own, qo_plane = lax.optimization_barrier((own, qo_plane))
    keys, values, local_state = keys_values_state(place, own, core_swap(send))

    qo = over_x(after(qo_plane, local_state))
    prior_state = gate(exchange(sums_of(exchange(local_state), False)))
    qo_near, own, send = project(
        place, (tokens, tokens_far, grads_in, grads_far), qo, dps, F32
    )
    recv = after(core_swap(send), prior_state)
    queries, scores, attn_grad, local_grad = attention_grad(
        place, own, recv, keys, values, prior_state, norm_gain.reshape(1, head)
    )
    kv_far = core_swap(kv_near)
    grad_pieces = exchange(local_grad)
    qo_far = core_swap(qo_near)
    base, *grads = inner_grads(
        place, queries, keys, values, scores, attn_grad, prior_state, qo_near, qo_far
    )
    later_state = exchange(sums_of(grad_pieces, True))
    result = output(place, base, *grads, keys, values, later_state, kv_near, kv_far)
    return result[None]


def solution(mesh):
    split = Mesh(mesh.devices.reshape(mesh.shape["dp"], 4, 8, 2), DP_SEQ)
    in_specs = (P("dp", SEQ, None), P(DP_SEQ, None, None), P(DP_SEQ, None), P(), P("dp", SEQ, None))
    out_specs = P("dp", SEQ, None)
    return jax.shard_map(
        per_device, mesh=split, in_specs=in_specs, out_specs=out_specs, check_vma=False
    )
```

```python
import functools

import jax
import jax.numpy as jnp
from jax import lax
from jax.experimental import pallas as pl
from jax.experimental.pallas import tpu as pltpu
from jax.sharding import Mesh
from jax.sharding import PartitionSpec as P

SEQ = ("x", "z", "core")
DP_SEQ = ("dp", "x", "z", "core")
ROWS = ("dp", "z")
BF16 = jnp.bfloat16
F32 = jnp.float32
LIMIT = 16 * 1024 * 1024
LONG = 30_000_000_000
SMEM = pl.BlockSpec(memory_space=pltpu.SMEM)
VMEM = pl.BlockSpec(memory_space=pltpu.VMEM)


def contract(left, right, left_dim, right_dim):
    return lax.dot_general(
        left, right, (((left_dim,), (right_dim,)), ((), ())), preferred_element_type=F32
    )


def cost(flops, moved):
    return pl.CostEstimate(flops=flops, bytes_accessed=moved, transcendentals=0)


def after(value, *events):
    return lax.optimization_barrier((value, *events))[0]


def core_swap(block):
    return lax.ppermute(block, "core", [(0, 1), (1, 0)])


def in_hbm(*values):
    return [pltpu.with_memory_space_constraint(v, pltpu.HBM) for v in values]


def in_vmem(*values):
    return [pltpu.with_memory_space_constraint(v, pltpu.VMEM) for v in values]


def project_kernel(shifts, steps, place_ref, *refs):
    tokens, blocks, (weight_ref, own_ref, send_ref, owns, sends) = refs[:-9], refs[-9:-5], refs[-5:]
    step = pl.program_id(0)
    depth = tokens[0].shape[1]
    rows = depth // 8

    @pl.when(step == 0)
    def _():
        owns[...] = jnp.zeros_like(owns)
        sends[...] = jnp.zeros_like(sends)

    for k, ref in zip(shifts, blocks):
        source = lax.rem(place_ref[0] - k + 4, 4)
        for p in range(2):
            at = pl.multiple_of(step * depth + (p * 4 + source) * rows, 64)
            weight_ref[pl.ds(at, rows), :] = ref[p * rows : (p + 1) * rows, :]

    weight = weight_ref[pl.ds(pl.multiple_of(step * depth, 128), depth), :]

    def products(own, far):
        owns[...] += contract(own[...], weight, 1, 0)
        sends[...] += contract(far[...], weight, 1, 0)

    if len(tokens) == 2:
        products(*tokens)
    else:
        pl.when(place_ref[1] == 0)(lambda: products(*tokens[:2]))
        pl.when(place_ref[1] != 0)(lambda: products(*tokens[2:]))

    @pl.when(step == steps - 1)
    def _():
        own_ref[...] = owns[...].astype(own_ref.dtype)
        send_ref[...] = sends[...].astype(send_ref.dtype)


def project(place, tokens, blocks, dtype):
    count, depth = tokens[0].shape
    steps = 4
    wide = (count, depth // steps)
    if len(tokens) == 2:
        pairs = [pl.BlockSpec(wide, lambda i, s: (0, i))] * 2
    else:
        pairs = [pl.BlockSpec(wide, lambda i, s: (0, i * (1 - s[1])))] * 2
        pairs += [pl.BlockSpec(wide, lambda i, s: (0, i * s[1]))] * 2
    weight = pl.BlockSpec((depth // 4 // steps, 128), lambda i, s: (i, 0))
    return pl.pallas_call(
        functools.partial(project_kernel, tuple(blocks), steps),
        out_shape=[pltpu.VMEM((depth, 128), BF16), *[pltpu.VMEM((count, 128), dtype)] * 2],
        grid_spec=pltpu.PrefetchScalarGridSpec(
            num_scalar_prefetch=1,
            grid=(steps,),
            in_specs=pairs + [weight] * 4,
            out_specs=[VMEM] * 3,
            scratch_shapes=[pltpu.VMEM((count, 128), F32)] * 2,
        ),
        compiler_params=pltpu.CompilerParams(vmem_limit_bytes=LIMIT),
        cost_estimate=cost(LONG, 4 * count * depth + 4 * depth * 128),
    )(place, *in_hbm(*tokens), *blocks.values())


def state_kernel(place_ref, own_ref, recv_ref, key_ref, value_ref, state_ref):
    own, recv = own_ref[...], recv_ref[...]
    first = place_ref[1] == 0
    keys, values = jnp.where(first, own, recv), jnp.where(first, recv, own)
    key_ref[...] = keys
    value_ref[...] = values
    state_ref[...] = contract(keys, values, 0, 0).astype(BF16)


def keys_values_state(place, own, recv):
    row = pltpu.VMEM(own.shape, BF16)
    return pl.pallas_call(
        state_kernel,
        out_shape=[row, row, jax.ShapeDtypeStruct((128, 128), BF16)],
        in_specs=[SMEM] + [VMEM] * 2,
        out_specs=[VMEM] * 3,
        compiler_params=pltpu.CompilerParams(vmem_limit_bytes=LIMIT),
        cost_estimate=cost(2 * own.size * 128, 8 * own.size),
    )(place, *in_vmem(own), recv)


def gate_kernel(in_ref, out_ref):
    out_ref[...] = in_ref[...]


def gate(value):
    return pl.pallas_call(
        gate_kernel,
        out_shape=pltpu.VMEM(value.shape, value.dtype),
        in_specs=[VMEM],
        out_specs=VMEM,
        compiler_params=pltpu.CompilerParams(vmem_limit_bytes=LIMIT),
        cost_estimate=cost(LONG, 4 * value.size),
    )(value)


def causal_of(count):
    rows = lax.broadcasted_iota(jnp.int32, (count, count), 0)
    return rows >= lax.broadcasted_iota(jnp.int32, (count, count), 1)


def grad_kernel(
    place_ref, near_ref, far_ref, k_ref, v_ref, prior_ref, gain_ref,
    q_ref, attn_ref, state_ref,
):
    first = place_ref[1] == 0
    near, far = near_ref[...], far_ref[...]
    queries = jnp.where(first, near, far).astype(BF16)
    head_grad = jnp.where(first, far, near)
    q_ref[...] = queries
    scores = contract(queries, k_ref[...], 1, 1)
    scores = jnp.where(causal_of(scores.shape[0]), scores, 0.0).astype(BF16)
    attended = contract(scores, v_ref[...], 1, 0) + contract(queries, prior_ref[...], 1, 0)
    inv_rms = lax.rsqrt(jnp.mean(attended * attended, axis=-1, keepdims=True) + 1e-06)
    scaled = gain_ref[...] * head_grad
    mean = jnp.mean(attended * scaled, axis=-1, keepdims=True)
    attn_grad = inv_rms * scaled - attended * (inv_rms * inv_rms * inv_rms) * mean
    attn_grad = attn_grad.astype(BF16)
    attn_ref[...] = attn_grad
    state_ref[...] = contract(queries, attn_grad, 0, 0).astype(BF16)


def attention_grad(place, near, far, keys, values, prior, gain):
    count = keys.shape[0]
    row = pltpu.VMEM((count, 128), BF16)
    return pl.pallas_call(
        grad_kernel,
        out_shape=[
            row,
            row,
            jax.ShapeDtypeStruct((128, 128), BF16),
        ],
        in_specs=[SMEM] + [VMEM] * 6,
        out_specs=[VMEM] * 3,
        compiler_params=pltpu.CompilerParams(vmem_limit_bytes=LIMIT),
        cost_estimate=cost(LONG, 16 * count * 128),
    )(place, *in_vmem(near), far, *in_vmem(keys, values, prior), gain)


def inner_kernel(
    place_ref, q_ref, k_ref, v_ref, attn_ref, prior_ref, near_ref, far_ref,
    base_ref, dk_ref, dv_ref,
):
    attn_grad = attn_ref[...]
    scores = contract(q_ref[...], k_ref[...], 1, 1)
    scores = jnp.where(causal_of(scores.shape[0]), scores, 0.0).astype(BF16)
    prob = contract(attn_grad, v_ref[...], 1, 1)
    prob = jnp.where(causal_of(prob.shape[0]), prob, 0.0).astype(BF16)
    query_grad = contract(prob, k_ref[...], 1, 0) + contract(attn_grad, prior_ref[...], 1, 1)
    query_grad = query_grad.astype(BF16)
    dk_ref[...] = contract(prob, q_ref[...], 0, 0)
    dv_ref[...] = contract(scores, attn_grad, 0, 0)
    part = near_ref.shape[0] // 4
    for i in range(4):
        at = slice(i * part, (i + 1) * part)
        weight = jnp.where(place_ref[1] == 0, near_ref[at, :], far_ref[at, :])
        base_ref[:, at] = contract(query_grad, weight, 1, 1)


def inner_grads(place, queries, keys, values, attn_grad, prior, near, far):
    count, depth = queries.shape[0], near.shape[0]
    return pl.pallas_call(
        inner_kernel,
        out_shape=[
            pltpu.VMEM((count, depth), F32),
            pltpu.VMEM((count, 128), F32),
            pltpu.VMEM((count, 128), F32),
        ],
        in_specs=[SMEM] + [VMEM] * 7,
        out_specs=[VMEM] * 3,
        compiler_params=pltpu.CompilerParams(vmem_limit_bytes=LIMIT),
        cost_estimate=cost(LONG, 4 * count * depth + 4 * depth * 128),
    )(place, *in_vmem(queries, keys, values, attn_grad, prior, near), far)


def output_kernel(place_ref, base, dk, dv, k_ref, v_ref, later, near_ref, far_ref, out_ref, joined):
    @pl.when(pl.program_id(0) == 0)
    def _():
        first = place_ref[1] == 0
        key_grad = (dk[...] + contract(v_ref[...], later[...], 1, 1)).astype(BF16)
        value_grad = (dv[...] + contract(k_ref[...], later[...], 1, 0)).astype(BF16)
        joined[:, :128] = jnp.where(first, key_grad, value_grad)
        joined[:, 128:] = jnp.where(first, value_grad, key_grad)

    part = out_ref.shape[1]
    at = pl.ds(pl.multiple_of(pl.program_id(0) * part, 128), part)
    weight = jnp.concatenate([near_ref[at, :], far_ref[at, :]], axis=1)
    total = base[:, at] + contract(joined[...], weight, 1, 1)
    out_ref[...] = total.astype(BF16)


def output(place, base, dk, dv, keys, values, later, near, far):
    count, depth = base.shape
    steps = 4
    return pl.pallas_call(
        output_kernel,
        grid=(steps,),
        out_shape=jax.ShapeDtypeStruct((count, depth), BF16),
        in_specs=[SMEM] + [VMEM] * 8,
        out_specs=pl.BlockSpec((count, depth // steps), lambda i: (0, i)),
        scratch_shapes=[pltpu.VMEM((count, 256), BF16)],
        compiler_params=pltpu.CompilerParams(vmem_limit_bytes=LIMIT),
        cost_estimate=cost(4 * count * depth * 128, 4 * depth * 128 + 6 * count * depth),
    )(place, *in_vmem(base, dk, dv, keys, values), later, *in_vmem(near), far)


def sums_kernel(reverse, in_ref, out_ref):
    each = in_ref.shape[0] // 64
    to = lax.broadcasted_iota(jnp.int32, (128, 128), 0)
    frm = lax.broadcasted_iota(jnp.int32, (128, 128), 1)
    others = (frm // each > to // each) if reverse else (frm // each < to // each)
    mask = jnp.where(others & (frm % each == to % each), 1.0, 0.0).astype(BF16)
    out_ref[...] = contract(mask, in_ref[...], 1, 0).astype(BF16)


def sums_of(pieces, reverse):
    return pl.pallas_call(
        functools.partial(sums_kernel, reverse),
        out_shape=jax.ShapeDtypeStruct(pieces.shape, BF16),
        in_specs=[VMEM],
        out_specs=VMEM,
        compiler_params=pltpu.CompilerParams(vmem_limit_bytes=LIMIT),
        cost_estimate=cost(LONG, 4 * pieces.size),
    )(pieces)


def exchange(state):
    peers, head = lax.axis_size(SEQ), state.shape[1]
    pieces = state.reshape(peers, -1, head)
    return lax.all_to_all(pieces, SEQ, 0, 0, tiled=True).reshape(state.shape)


def per_device(inputs, w_project, w_output, norm_gain, out_grad):
    tokens = inputs[0]
    grads_in = out_grad[0]
    head = w_output.shape[1]
    dps, zs, xs = lax.axis_size("dp"), lax.axis_size("z"), lax.axis_size("x")
    place = jnp.stack([lax.axis_index("x"), lax.axis_index("core")]).astype(jnp.int32)
    on_first = lax.axis_index("core") == 0

    rows = jnp.concatenate([w_project.reshape(-1, 3 * head), w_output], axis=1)
    rows = lax.all_gather(rows, "core", axis=0, tiled=True)
    kv_rows = jnp.where(on_first, rows[:, head : 2 * head], rows[:, 2 * head : 3 * head])
    qo_rows = jnp.where(on_first, rows[:, :head], rows[:, 3 * head :])

    def copied(block):
        return jnp.broadcast_to(block[None], (dps * zs, *block.shape))

    def over_planes(copies):
        return lax.all_to_all(copies, ROWS, 0, 0, tiled=True).reshape(-1, head)

    def over_x(block):
        shifts = {k: lax.ppermute(block, "x", [(i, (i + k) % xs) for i in range(xs)]) for k in (2, 1, 3)}
        return {1: shifts[1], 3: shifts[3], 2: shifts[2], 0: block}

    kv_copies = copied(kv_rows)
    tokens_far = core_swap(after(tokens, kv_copies))
    grads_far = core_swap(after(grads_in, kv_copies))
    kv_plane = over_planes(kv_copies)
    qo_plane = over_planes(copied(gate(after(qo_rows, kv_plane))))
    tokens_far = after(tokens_far, grads_far)
    kv_near, own, send = project(place, (tokens, tokens_far), over_x(kv_plane), BF16)
    own, qo_plane = lax.optimization_barrier((own, qo_plane))
    keys, values, local_state = keys_values_state(place, own, core_swap(send))

    qo = over_x(after(qo_plane, local_state))
    prior_state = gate(exchange(sums_of(exchange(local_state), False)))
    qo_near, own, send = project(
        place, (tokens, tokens_far, grads_in, grads_far), qo, F32
    )
    recv = after(core_swap(send), prior_state)
    queries, attn_grad, local_grad = attention_grad(
        place, own, recv, keys, values, prior_state, norm_gain.reshape(1, head)
    )
    kv_far = core_swap(kv_near)
    grad_pieces = exchange(local_grad)
    qo_far = core_swap(qo_near)
    base, *grads = inner_grads(
        place, queries, keys, values, attn_grad, prior_state, qo_near, qo_far
    )
    later_state = exchange(sums_of(grad_pieces, True))
    result = output(place, base, *grads, keys, values, later_state, kv_near, kv_far)
    return result[None]


def solution(mesh):
    split = Mesh(mesh.devices.reshape(mesh.shape["dp"], 4, 8, 2), DP_SEQ)
    in_specs = (P("dp", SEQ, None), P(DP_SEQ, None, None), P(DP_SEQ, None), P(), P("dp", SEQ, None))
    out_specs = P("dp", SEQ, None)
    return jax.shard_map(
        per_device, mesh=split, in_specs=in_specs, out_specs=out_specs, check_vma=False
    )
```

```python
import functools

import jax
import jax.numpy as jnp
from jax import lax
from jax.experimental import pallas as pl
from jax.experimental.pallas import tpu as pltpu
from jax.sharding import Mesh
from jax.sharding import PartitionSpec as P

SEQ = ("x", "z", "core")
DP_SEQ = ("dp", "x", "z", "core")
ROWS = ("dp", "z")
BF16 = jnp.bfloat16
F32 = jnp.float32
LIMIT = 16 * 1024 * 1024
LONG = 30_000_000_000
SMEM = pl.BlockSpec(memory_space=pltpu.SMEM)
VMEM = pl.BlockSpec(memory_space=pltpu.VMEM)


def contract(left, right, left_dim, right_dim):
    return lax.dot_general(
        left, right, (((left_dim,), (right_dim,)), ((), ())), preferred_element_type=F32
    )


def cost(flops, moved):
    return pl.CostEstimate(flops=flops, bytes_accessed=moved, transcendentals=0)


def after(value, *events):
    return lax.optimization_barrier((value, *events))[0]


def core_swap(block):
    return lax.ppermute(block, "core", [(0, 1), (1, 0)])


def in_hbm(*values):
    return [pltpu.with_memory_space_constraint(v, pltpu.HBM) for v in values]


def project_kernel(shifts, place_ref, *refs):
    tokens, blocks, outs, scratch = refs[:-11], refs[-11:-7], refs[-7:-4], refs[-4:]
    weight_ref, own_ref, send_ref = outs
    own_held, far_held, own_sem, far_sem = scratch
    rows = weight_ref.shape[0] // 32

    def products(own, far):
        own_copy = pltpu.make_async_copy(own, own_held, own_sem)
        far_copy = pltpu.make_async_copy(far, far_held, far_sem)
        own_copy.start()
        far_copy.start()
        for k, ref in zip(shifts, blocks):
            source = lax.rem(place_ref[0] - k + 4, 4)
            for p in range(8):
                at = pl.multiple_of((p * 4 + source) * rows, 64)
                weight_ref[pl.ds(at, rows), :] = ref[p * rows : (p + 1) * rows, :]
        own_copy.wait()
        own_ref[...] = contract(own_held[...], weight_ref[...], 1, 0).astype(own_ref.dtype)
        far_copy.wait()
        send_ref[...] = contract(far_held[...], weight_ref[...], 1, 0).astype(send_ref.dtype)

    if len(tokens) == 2:
        products(*tokens)
    else:
        pl.when(place_ref[1] == 0)(lambda: products(*tokens[:2]))
        pl.when(place_ref[1] != 0)(lambda: products(*tokens[2:]))


def project(place, tokens, blocks, dtype):
    count, depth = tokens[0].shape
    row = jax.ShapeDtypeStruct((count, 128), dtype)
    return pl.pallas_call(
        functools.partial(project_kernel, tuple(blocks)),
        out_shape=[jax.ShapeDtypeStruct((depth, 128), BF16), row, row],
        in_specs=[SMEM] + [pl.BlockSpec(memory_space=pl.ANY)] * len(tokens) + [VMEM] * 4,
        out_specs=[VMEM] * 3,
        scratch_shapes=[pltpu.VMEM((count, depth), BF16)] * 2 + [pltpu.SemaphoreType.DMA] * 2,
        compiler_params=pltpu.CompilerParams(vmem_limit_bytes=LIMIT),
        cost_estimate=cost(LONG, 4 * count * depth + 4 * depth * 128),
    )(place, *in_hbm(*tokens), *blocks.values())


def state_kernel(place_ref, own_ref, recv_ref, key_ref, value_ref, state_ref):
    own, recv = own_ref[...], recv_ref[...]
    first = place_ref[1] == 0
    keys, values = jnp.where(first, own, recv), jnp.where(first, recv, own)
    key_ref[...] = keys
    value_ref[...] = values
    state_ref[...] = contract(keys, values, 0, 0).astype(BF16)


def keys_values_state(place, own, recv):
    row = jax.ShapeDtypeStruct(own.shape, BF16)
    return pl.pallas_call(
        state_kernel,
        out_shape=[row, row, jax.ShapeDtypeStruct((128, 128), BF16)],
        in_specs=[SMEM] + [VMEM] * 2,
        out_specs=[VMEM] * 3,
        compiler_params=pltpu.CompilerParams(vmem_limit_bytes=LIMIT),
        cost_estimate=cost(2 * own.size * 128, 8 * own.size),
    )(place, own, recv)


def gate_kernel(in_ref, out_ref):
    out_ref[...] = in_ref[...]


def gate(value):
    return pl.pallas_call(
        gate_kernel,
        out_shape=jax.ShapeDtypeStruct(value.shape, value.dtype),
        in_specs=[VMEM],
        out_specs=VMEM,
        compiler_params=pltpu.CompilerParams(vmem_limit_bytes=LIMIT),
        cost_estimate=cost(LONG, 4 * value.size),
    )(value)


def causal_of(count):
    rows = lax.broadcasted_iota(jnp.int32, (count, count), 0)
    return rows >= lax.broadcasted_iota(jnp.int32, (count, count), 1)


def grad_kernel(
    place_ref, near_ref, far_ref, k_ref, v_ref, prior_ref, gain_ref,
    q_ref, attn_ref, state_ref,
):
    first = place_ref[1] == 0
    near, far = near_ref[...], far_ref[...]
    queries = jnp.where(first, near, far).astype(BF16)
    head_grad = jnp.where(first, far, near)
    q_ref[...] = queries
    scores = contract(queries, k_ref[...], 1, 1)
    scores = jnp.where(causal_of(scores.shape[0]), scores, 0.0).astype(BF16)
    attended = contract(scores, v_ref[...], 1, 0) + contract(queries, prior_ref[...], 1, 0)
    inv_rms = lax.rsqrt(jnp.mean(attended * attended, axis=-1, keepdims=True) + 1e-06)
    scaled = gain_ref[...] * head_grad
    mean = jnp.mean(attended * scaled, axis=-1, keepdims=True)
    attn_grad = inv_rms * scaled - attended * (inv_rms * inv_rms * inv_rms) * mean
    attn_grad = attn_grad.astype(BF16)
    attn_ref[...] = attn_grad
    state_ref[...] = contract(queries, attn_grad, 0, 0).astype(BF16)


def attention_grad(place, near, far, keys, values, prior, gain):
    count = keys.shape[0]
    row = jax.ShapeDtypeStruct((count, 128), BF16)
    return pl.pallas_call(
        grad_kernel,
        out_shape=[
            row,
            row,
            jax.ShapeDtypeStruct((128, 128), BF16),
        ],
        in_specs=[SMEM] + [VMEM] * 6,
        out_specs=[VMEM] * 3,
        compiler_params=pltpu.CompilerParams(vmem_limit_bytes=LIMIT),
        cost_estimate=cost(LONG, 16 * count * 128),
    )(place, near, far, keys, values, prior, gain)


def inner_kernel(place_ref, *refs):
    rows_any, (near_any, far_any), outs, scratch = refs[:5], refs[5:7], refs[7:10], refs[10:]
    base_ref, dk_ref, dv_ref = outs
    q_ref, k_ref, v_ref, attn_ref, prior_ref, weight_ref, row_sems, weight_sem = scratch

    def body(weight_any):
        weight_copy = pltpu.make_async_copy(weight_any, weight_ref, weight_sem)
        copies = [
            pltpu.make_async_copy(source, target, row_sems.at[i])
            for i, (source, target) in enumerate(zip(rows_any, scratch[:5]))
        ]
        for copy in copies:
            copy.start()
        weight_copy.start()
        for copy in copies:
            copy.wait()
        attn_grad = attn_ref[...]
        causal = causal_of(attn_grad.shape[0])
        scores = contract(q_ref[...], k_ref[...], 1, 1)
        scores = jnp.where(causal, scores, 0.0).astype(BF16)
        prob = contract(attn_grad, v_ref[...], 1, 1)
        prob = jnp.where(causal, prob, 0.0).astype(BF16)
        query_grad = contract(prob, k_ref[...], 1, 0) + contract(attn_grad, prior_ref[...], 1, 1)
        query_grad = query_grad.astype(BF16)
        dk_ref[...] = contract(prob, q_ref[...], 0, 0)
        dv_ref[...] = contract(scores, attn_grad, 0, 0)
        weight_copy.wait()
        part = weight_ref.shape[0] // 4
        for i in range(4):
            at = slice(i * part, (i + 1) * part)
            base_ref[:, at] = contract(query_grad, weight_ref[at, :], 1, 1)

    pl.when(place_ref[1] == 0)(lambda: body(near_any))
    pl.when(place_ref[1] != 0)(lambda: body(far_any))


def inner_grads(place, queries, keys, values, attn_grad, prior, near, far):
    count, depth = queries.shape[0], near.shape[0]
    row = pltpu.VMEM((count, 128), BF16)
    return pl.pallas_call(
        inner_kernel,
        out_shape=[
            jax.ShapeDtypeStruct((count, depth), F32),
            jax.ShapeDtypeStruct((count, 128), F32),
            jax.ShapeDtypeStruct((count, 128), F32),
        ],
        in_specs=[SMEM] + [pl.BlockSpec(memory_space=pl.ANY)] * 7,
        out_specs=[VMEM] * 3,
        scratch_shapes=[
            *[row] * 4,
            pltpu.VMEM((128, 128), BF16),
            pltpu.VMEM((depth, 128), BF16),
            pltpu.SemaphoreType.DMA((5,)),
            pltpu.SemaphoreType.DMA,
        ],
        compiler_params=pltpu.CompilerParams(vmem_limit_bytes=LIMIT),
        cost_estimate=cost(LONG, 4 * count * depth + 4 * depth * 128),
    )(place, *in_hbm(queries, keys, values, attn_grad, prior, near, far))


def output_kernel(
    place_ref, base, dk, dv, k_any, v_any, later, near_any, far_any, out_any,
    k_ref, v_ref, near_ref, far_ref, out_ref, row_sems, weight_sems, out_sems,
):
    steps, _, part = out_ref.shape
    rows = [
        pltpu.make_async_copy(k_any, k_ref, row_sems.at[0]),
        pltpu.make_async_copy(v_any, v_ref, row_sems.at[1]),
    ]
    weights = []
    for i in range(steps):
        at = pl.ds(i * part, part)
        for n, (source, target) in enumerate(((near_any, near_ref), (far_any, far_ref))):
            weights.append(
                pltpu.make_async_copy(source.at[at], target.at[at], weight_sems.at[2 * i + n])
            )
    for copy in rows + weights:
        copy.start()
    for copy in rows:
        copy.wait()
    first = place_ref[1] == 0
    key_grad = (dk[...] + contract(v_ref[...], later[...], 1, 1)).astype(BF16)
    value_grad = (dv[...] + contract(k_ref[...], later[...], 1, 0)).astype(BF16)
    near_grad = jnp.where(first, key_grad, value_grad)
    far_grad = jnp.where(first, value_grad, key_grad)
    joined = jnp.concatenate([near_grad, far_grad], axis=1)
    outs = []
    for i in range(steps):
        weights[2 * i].wait()
        weights[2 * i + 1].wait()
        at = slice(i * part, (i + 1) * part)
        weight = jnp.concatenate([near_ref[at, :], far_ref[at, :]], axis=1)
        out_ref[i] = (base[:, at] + contract(joined, weight, 1, 1)).astype(BF16)
        copy = pltpu.make_async_copy(
            out_ref.at[i], out_any.at[:, pl.ds(i * part, part)], out_sems.at[i]
        )
        copy.start()
        outs.append(copy)
    for copy in outs:
        copy.wait()


def output(place, base, dk, dv, keys, values, later, near, far):
    count, depth = base.shape
    steps = 4
    anywhere = pl.BlockSpec(memory_space=pl.ANY)
    return pl.pallas_call(
        output_kernel,
        out_shape=jax.ShapeDtypeStruct((count, depth), BF16),
        in_specs=[SMEM] + [VMEM] * 3 + [anywhere] * 2 + [VMEM] + [anywhere] * 2,
        out_specs=anywhere,
        scratch_shapes=[
            pltpu.VMEM((count, 128), BF16),
            pltpu.VMEM((count, 128), BF16),
            pltpu.VMEM((depth, 128), BF16),
            pltpu.VMEM((depth, 128), BF16),
            pltpu.VMEM((steps, count, depth // steps), BF16),
            pltpu.SemaphoreType.DMA((2,)),
            pltpu.SemaphoreType.DMA((2 * steps,)),
            pltpu.SemaphoreType.DMA((steps,)),
        ],
        compiler_params=pltpu.CompilerParams(vmem_limit_bytes=LIMIT),
        cost_estimate=cost(4 * count * depth * 128, 4 * depth * 128 + 6 * count * depth),
    )(place, base, dk, dv, *in_hbm(keys, values), later, *in_hbm(near, far))


def sums_kernel(reverse, in_ref, out_ref):
    each = in_ref.shape[0] // 64
    to = lax.broadcasted_iota(jnp.int32, (128, 128), 0)
    frm = lax.broadcasted_iota(jnp.int32, (128, 128), 1)
    others = (frm // each > to // each) if reverse else (frm // each < to // each)
    mask = jnp.where(others & (frm % each == to % each), 1.0, 0.0).astype(BF16)
    out_ref[...] = contract(mask, in_ref[...], 1, 0).astype(BF16)


def sums_of(pieces, reverse):
    return pl.pallas_call(
        functools.partial(sums_kernel, reverse),
        out_shape=jax.ShapeDtypeStruct(pieces.shape, BF16),
        in_specs=[VMEM],
        out_specs=VMEM,
        compiler_params=pltpu.CompilerParams(vmem_limit_bytes=LIMIT),
        cost_estimate=cost(LONG, 4 * pieces.size),
    )(pieces)


def exchange(state):
    peers, head = lax.axis_size(SEQ), state.shape[1]
    pieces = state.reshape(peers, -1, head)
    return lax.all_to_all(pieces, SEQ, 0, 0, tiled=True).reshape(state.shape)


def per_device(inputs, w_project, w_output, norm_gain, out_grad):
    tokens = inputs[0]
    grads_in = out_grad[0]
    head = w_output.shape[1]
    dps, zs, xs = lax.axis_size("dp"), lax.axis_size("z"), lax.axis_size("x")
    place = jnp.stack([lax.axis_index("x"), lax.axis_index("core")]).astype(jnp.int32)
    on_first = lax.axis_index("core") == 0

    rows = jnp.concatenate([w_project.reshape(-1, 3 * head), w_output], axis=1)
    rows = lax.all_gather(rows, "core", axis=0, tiled=True)
    kv_rows = jnp.where(on_first, rows[:, head : 2 * head], rows[:, 2 * head : 3 * head])
    qo_rows = jnp.where(on_first, rows[:, :head], rows[:, 3 * head :])

    def copied(block):
        return jnp.broadcast_to(block[None], (dps * zs, *block.shape))

    def over_planes(copies):
        return lax.all_to_all(copies, ROWS, 0, 0, tiled=True).reshape(-1, head)

    def over_x(block):
        shifts = {k: lax.ppermute(block, "x", [(i, (i + k) % xs) for i in range(xs)]) for k in (2, 1, 3)}
        return {1: shifts[1], 3: shifts[3], 2: shifts[2], 0: block}

    kv_copies = copied(kv_rows)
    tokens_far = core_swap(after(tokens, kv_copies))
    grads_far = core_swap(after(grads_in, kv_copies))
    kv_plane = over_planes(kv_copies)
    qo_plane = over_planes(copied(gate(after(qo_rows, kv_plane))))
    tokens_far = after(tokens_far, grads_far)
    kv_near, own, send = project(place, (tokens, tokens_far), over_x(kv_plane), BF16)
    own, qo_plane = lax.optimization_barrier((own, qo_plane))
    keys, values, local_state = keys_values_state(place, own, core_swap(send))

    qo = over_x(after(qo_plane, local_state))
    prior_state = gate(exchange(sums_of(exchange(local_state), False)))
    qo_near, own, send = project(
        place, (tokens, tokens_far, grads_in, grads_far), qo, F32
    )
    recv = after(core_swap(send), prior_state)
    queries, attn_grad, local_grad = attention_grad(
        place, own, recv, keys, values, prior_state, norm_gain.reshape(1, head)
    )
    kv_far = core_swap(kv_near)
    grad_pieces = exchange(local_grad)
    qo_far = core_swap(qo_near)
    base, *grads = inner_grads(
        place, queries, keys, values, attn_grad, prior_state, qo_near, qo_far
    )
    later_state = exchange(sums_of(grad_pieces, True))
    result = output(place, base, *grads, keys, values, later_state, kv_near, kv_far)
    return result[None]


def solution(mesh):
    split = Mesh(mesh.devices.reshape(mesh.shape["dp"], 4, 8, 2), DP_SEQ)
    in_specs = (P("dp", SEQ, None), P(DP_SEQ, None, None), P(DP_SEQ, None), P(), P("dp", SEQ, None))
    out_specs = P("dp", SEQ, None)
    return jax.shard_map(
        per_device, mesh=split, in_specs=in_specs, out_specs=out_specs, check_vma=False
    )
```

```python
import functools

import jax
import jax.numpy as jnp
from jax import lax
from jax.experimental import pallas as pl
from jax.experimental.pallas import tpu as pltpu
from jax.sharding import Mesh
from jax.sharding import PartitionSpec as P

SEQ = ("x", "z", "core")
DP_SEQ = ("dp", "x", "z", "core")
ROWS = ("dp", "z")
BF16 = jnp.bfloat16
F32 = jnp.float32
LIMIT = 16 * 1024 * 1024
LONG = 30_000_000_000
SMEM = pl.BlockSpec(memory_space=pltpu.SMEM)
VMEM = pl.BlockSpec(memory_space=pltpu.VMEM)


def contract(left, right, left_dim, right_dim):
    return lax.dot_general(
        left, right, (((left_dim,), (right_dim,)), ((), ())), preferred_element_type=F32
    )


def cost(flops, moved):
    return pl.CostEstimate(flops=flops, bytes_accessed=moved, transcendentals=0)


def after(value, *events):
    return lax.optimization_barrier((value, *events))[0]


def core_swap(block):
    return lax.ppermute(block, "core", [(0, 1), (1, 0)])


def in_hbm(*values):
    return [pltpu.with_memory_space_constraint(v, pltpu.HBM) for v in values]


def project_kernel(shifts, place_ref, *refs):
    tokens, blocks, outs, scratch = refs[:-11], refs[-11:-7], refs[-7:-4], refs[-4:]
    weight_ref, own_ref, send_ref = outs
    own_held, far_held, row_sems, block_sems = scratch
    dps, xs, rows, head = weight_ref.shape

    def products(own, far):
        row_copies = [
            pltpu.make_async_copy(own, own_held, row_sems.at[0]),
            pltpu.make_async_copy(far, far_held, row_sems.at[1]),
        ]
        block_copies = []
        for i, (k, ref) in enumerate(zip(shifts, blocks)):
            source = lax.rem(place_ref[0] - k + xs, xs)
            block_copies.append(
                pltpu.make_async_copy(ref, weight_ref.at[:, source], block_sems.at[i])
            )
        for copy in block_copies + row_copies:
            copy.start()
        for copy in block_copies + row_copies[:1]:
            copy.wait()
        weight = weight_ref[...].reshape(dps * xs * rows, head)
        own_ref[...] = contract(own_held[...], weight, 1, 0).astype(own_ref.dtype)
        row_copies[1].wait()
        send_ref[...] = contract(far_held[...], weight, 1, 0).astype(send_ref.dtype)

    if len(tokens) == 2:
        products(*tokens)
    else:
        pl.when(place_ref[1] == 0)(lambda: products(*tokens[:2]))
        pl.when(place_ref[1] != 0)(lambda: products(*tokens[2:]))


def project(place, tokens, blocks, dtype):
    count, depth = tokens[0].shape
    dps, xs = lax.axis_size("dp"), len(blocks)
    rows = depth // (dps * xs)
    row = jax.ShapeDtypeStruct((count, 128), dtype)
    weight, own, send = pl.pallas_call(
        functools.partial(project_kernel, tuple(blocks)),
        out_shape=[jax.ShapeDtypeStruct((dps, xs, rows, 128), BF16), row, row],
        in_specs=[SMEM] + [pl.BlockSpec(memory_space=pl.ANY)] * (len(tokens) + xs),
        out_specs=[VMEM] * 3,
        scratch_shapes=[pltpu.VMEM((count, depth), BF16)] * 2
        + [pltpu.SemaphoreType.DMA((2,)), pltpu.SemaphoreType.DMA((xs,))],
        compiler_params=pltpu.CompilerParams(vmem_limit_bytes=LIMIT),
        cost_estimate=cost(LONG, 4 * count * depth + 4 * depth * 128),
    )(place, *in_hbm(*tokens), *in_hbm(*[v.reshape(dps, rows, 128) for v in blocks.values()]))
    return weight.reshape(depth, 128), own, send


def state_kernel(place_ref, own_ref, recv_ref, key_ref, value_ref, state_ref):
    own, recv = own_ref[...], recv_ref[...]
    first = place_ref[1] == 0
    keys, values = jnp.where(first, own, recv), jnp.where(first, recv, own)
    key_ref[...] = keys
    value_ref[...] = values
    state_ref[...] = contract(keys, values, 0, 0).astype(BF16)


def keys_values_state(place, own, recv):
    row = jax.ShapeDtypeStruct(own.shape, BF16)
    return pl.pallas_call(
        state_kernel,
        out_shape=[row, row, jax.ShapeDtypeStruct((128, 128), BF16)],
        in_specs=[SMEM] + [VMEM] * 2,
        out_specs=[VMEM] * 3,
        compiler_params=pltpu.CompilerParams(vmem_limit_bytes=LIMIT),
        cost_estimate=cost(2 * own.size * 128, 8 * own.size),
    )(place, own, recv)


def gate_kernel(in_ref, out_ref):
    out_ref[...] = in_ref[...]


def gate(value):
    return pl.pallas_call(
        gate_kernel,
        out_shape=jax.ShapeDtypeStruct(value.shape, value.dtype),
        in_specs=[VMEM],
        out_specs=VMEM,
        compiler_params=pltpu.CompilerParams(vmem_limit_bytes=LIMIT),
        cost_estimate=cost(LONG, 4 * value.size),
    )(value)


def causal_of(count):
    rows = lax.broadcasted_iota(jnp.int32, (count, count), 0)
    return rows >= lax.broadcasted_iota(jnp.int32, (count, count), 1)


def grad_kernel(
    place_ref, near_ref, far_ref, k_ref, v_ref, prior_ref, gain_ref,
    q_ref, attn_ref, state_ref,
):
    first = place_ref[1] == 0
    near, far = near_ref[...], far_ref[...]
    queries = jnp.where(first, near, far).astype(BF16)
    head_grad = jnp.where(first, far, near)
    q_ref[...] = queries
    scores = contract(queries, k_ref[...], 1, 1)
    scores = jnp.where(causal_of(scores.shape[0]), scores, 0.0).astype(BF16)
    attended = contract(scores, v_ref[...], 1, 0) + contract(queries, prior_ref[...], 1, 0)
    inv_rms = lax.rsqrt(jnp.mean(attended * attended, axis=-1, keepdims=True) + 1e-06)
    scaled = gain_ref[...] * head_grad
    mean = jnp.mean(attended * scaled, axis=-1, keepdims=True)
    attn_grad = inv_rms * scaled - attended * (inv_rms * inv_rms * inv_rms) * mean
    attn_grad = attn_grad.astype(BF16)
    attn_ref[...] = attn_grad
    state_ref[...] = contract(queries, attn_grad, 0, 0).astype(BF16)


def attention_grad(place, near, far, keys, values, prior, gain):
    count = keys.shape[0]
    row = jax.ShapeDtypeStruct((count, 128), BF16)
    return pl.pallas_call(
        grad_kernel,
        out_shape=[
            row,
            row,
            jax.ShapeDtypeStruct((128, 128), BF16),
        ],
        in_specs=[SMEM] + [VMEM] * 6,
        out_specs=[VMEM] * 3,
        compiler_params=pltpu.CompilerParams(vmem_limit_bytes=LIMIT),
        cost_estimate=cost(LONG, 16 * count * 128),
    )(place, near, far, keys, values, prior, gain)


def inner_kernel(place_ref, *refs):
    rows_any, (near_any, far_any), outs, scratch = refs[:5], refs[5:7], refs[7:10], refs[10:]
    base_ref, dk_ref, dv_ref = outs
    q_ref, k_ref, v_ref, attn_ref, prior_ref, weight_ref, row_sems, weight_sem = scratch

    def body(weight_any):
        weight_copy = pltpu.make_async_copy(weight_any, weight_ref, weight_sem)
        copies = [
            pltpu.make_async_copy(source, target, row_sems.at[i])
            for i, (source, target) in enumerate(zip(rows_any, scratch[:5]))
        ]
        for copy in copies:
            copy.start()
        weight_copy.start()
        for copy in copies:
            copy.wait()
        attn_grad = attn_ref[...]
        causal = causal_of(attn_grad.shape[0])
        scores = contract(q_ref[...], k_ref[...], 1, 1)
        scores = jnp.where(causal, scores, 0.0).astype(BF16)
        prob = contract(attn_grad, v_ref[...], 1, 1)
        prob = jnp.where(causal, prob, 0.0).astype(BF16)
        query_grad = contract(prob, k_ref[...], 1, 0) + contract(attn_grad, prior_ref[...], 1, 1)
        query_grad = query_grad.astype(BF16)
        dk_ref[...] = contract(prob, q_ref[...], 0, 0)
        dv_ref[...] = contract(scores, attn_grad, 0, 0)
        weight_copy.wait()
        part = weight_ref.shape[0] // 4
        for i in range(4):
            at = slice(i * part, (i + 1) * part)
            base_ref[:, at] = contract(query_grad, weight_ref[at, :], 1, 1)

    pl.when(place_ref[1] == 0)(lambda: body(near_any))
    pl.when(place_ref[1] != 0)(lambda: body(far_any))


def inner_grads(place, queries, keys, values, attn_grad, prior, near, far):
    count, depth = queries.shape[0], near.shape[0]
    row = pltpu.VMEM((count, 128), BF16)
    return pl.pallas_call(
        inner_kernel,
        out_shape=[
            jax.ShapeDtypeStruct((count, depth), F32),
            jax.ShapeDtypeStruct((count, 128), F32),
            jax.ShapeDtypeStruct((count, 128), F32),
        ],
        in_specs=[SMEM] + [pl.BlockSpec(memory_space=pl.ANY)] * 7,
        out_specs=[VMEM] * 3,
        scratch_shapes=[
            *[row] * 4,
            pltpu.VMEM((128, 128), BF16),
            pltpu.VMEM((depth, 128), BF16),
            pltpu.SemaphoreType.DMA((5,)),
            pltpu.SemaphoreType.DMA,
        ],
        compiler_params=pltpu.CompilerParams(vmem_limit_bytes=LIMIT),
        cost_estimate=cost(LONG, 4 * count * depth + 4 * depth * 128),
    )(place, *in_hbm(queries, keys, values, attn_grad, prior, near, far))


def output_kernel(
    place_ref, base, dk, dv, k_any, v_any, later, near_any, far_any, out_any,
    k_ref, v_ref, near_ref, far_ref, out_ref, row_sems, weight_sems, out_sems,
):
    steps, _, part = out_ref.shape
    rows = [
        pltpu.make_async_copy(k_any, k_ref, row_sems.at[0]),
        pltpu.make_async_copy(v_any, v_ref, row_sems.at[1]),
    ]
    weights = []
    for i in range(steps):
        at = pl.ds(i * part, part)
        for n, (source, target) in enumerate(((near_any, near_ref), (far_any, far_ref))):
            weights.append(
                pltpu.make_async_copy(source.at[at], target.at[at], weight_sems.at[2 * i + n])
            )
    for copy in rows + weights:
        copy.start()
    for copy in rows:
        copy.wait()
    first = place_ref[1] == 0
    key_grad = (dk[...] + contract(v_ref[...], later[...], 1, 1)).astype(BF16)
    value_grad = (dv[...] + contract(k_ref[...], later[...], 1, 0)).astype(BF16)
    near_grad = jnp.where(first, key_grad, value_grad)
    far_grad = jnp.where(first, value_grad, key_grad)
    joined = jnp.concatenate([near_grad, far_grad], axis=1)
    outs = []
    for i in range(steps):
        weights[2 * i].wait()
        weights[2 * i + 1].wait()
        at = slice(i * part, (i + 1) * part)
        weight = jnp.concatenate([near_ref[at, :], far_ref[at, :]], axis=1)
        out_ref[i] = (base[:, at] + contract(joined, weight, 1, 1)).astype(BF16)
        copy = pltpu.make_async_copy(
            out_ref.at[i], out_any.at[:, pl.ds(i * part, part)], out_sems.at[i]
        )
        copy.start()
        outs.append(copy)
    for copy in outs:
        copy.wait()


def output(place, base, dk, dv, keys, values, later, near, far):
    count, depth = base.shape
    steps = 4
    anywhere = pl.BlockSpec(memory_space=pl.ANY)
    return pl.pallas_call(
        output_kernel,
        out_shape=jax.ShapeDtypeStruct((count, depth), BF16),
        in_specs=[SMEM] + [VMEM] * 3 + [anywhere] * 2 + [VMEM] + [anywhere] * 2,
        out_specs=anywhere,
        scratch_shapes=[
            pltpu.VMEM((count, 128), BF16),
            pltpu.VMEM((count, 128), BF16),
            pltpu.VMEM((depth, 128), BF16),
            pltpu.VMEM((depth, 128), BF16),
            pltpu.VMEM((steps, count, depth // steps), BF16),
            pltpu.SemaphoreType.DMA((2,)),
            pltpu.SemaphoreType.DMA((2 * steps,)),
            pltpu.SemaphoreType.DMA((steps,)),
        ],
        compiler_params=pltpu.CompilerParams(vmem_limit_bytes=LIMIT),
        cost_estimate=cost(4 * count * depth * 128, 4 * depth * 128 + 6 * count * depth),
    )(place, base, dk, dv, *in_hbm(keys, values), later, *in_hbm(near, far))


def sums_kernel(reverse, in_ref, out_ref):
    each = in_ref.shape[0] // 64
    to = lax.broadcasted_iota(jnp.int32, (128, 128), 0)
    frm = lax.broadcasted_iota(jnp.int32, (128, 128), 1)
    others = (frm // each > to // each) if reverse else (frm // each < to // each)
    mask = jnp.where(others & (frm % each == to % each), 1.0, 0.0).astype(BF16)
    out_ref[...] = contract(mask, in_ref[...], 1, 0).astype(BF16)


def sums_of(pieces, reverse):
    return pl.pallas_call(
        functools.partial(sums_kernel, reverse),
        out_shape=jax.ShapeDtypeStruct(pieces.shape, BF16),
        in_specs=[VMEM],
        out_specs=VMEM,
        compiler_params=pltpu.CompilerParams(vmem_limit_bytes=LIMIT),
        cost_estimate=cost(LONG, 4 * pieces.size),
    )(pieces)


def exchange(state):
    peers, head = lax.axis_size(SEQ), state.shape[1]
    pieces = state.reshape(peers, -1, head)
    return lax.all_to_all(pieces, SEQ, 0, 0, tiled=True).reshape(state.shape)


def per_device(inputs, w_project, w_output, norm_gain, out_grad):
    tokens = inputs[0]
    grads_in = out_grad[0]
    head = w_output.shape[1]
    dps, zs, xs = lax.axis_size("dp"), lax.axis_size("z"), lax.axis_size("x")
    place = jnp.stack([lax.axis_index("x"), lax.axis_index("core")]).astype(jnp.int32)
    on_first = lax.axis_index("core") == 0

    rows = jnp.concatenate([w_project.reshape(-1, 3 * head), w_output], axis=1)
    rows = lax.all_gather(rows, "core", axis=0, tiled=True)
    kv_rows = jnp.where(on_first, rows[:, head : 2 * head], rows[:, 2 * head : 3 * head])
    qo_rows = jnp.where(on_first, rows[:, :head], rows[:, 3 * head :])

    def copied(block):
        return jnp.broadcast_to(block[None], (dps * zs, *block.shape))

    def over_planes(copies):
        return lax.all_to_all(copies, ROWS, 0, 0, tiled=True).reshape(-1, head)

    def over_x(block):
        shifts = {k: lax.ppermute(block, "x", [(i, (i + k) % xs) for i in range(xs)]) for k in (2, 1, 3)}
        return {1: shifts[1], 3: shifts[3], 2: shifts[2], 0: block}

    kv_copies, qo_copies = copied(kv_rows), copied(qo_rows)
    tokens_far = core_swap(after(tokens, kv_copies))
    grads_far = core_swap(after(grads_in, kv_copies))
    kv_plane = gate(over_planes(kv_copies))
    qo_plane = gate(over_planes(after(qo_copies, kv_plane, tokens_far, grads_far)))
    kv, qo = over_x(kv_plane), over_x(qo_plane)
    kv_near, own, send = project(place, (tokens, tokens_far), kv, BF16)
    keys, values, local_state = keys_values_state(place, own, core_swap(send))

    pieces = exchange(local_state)
    qo_near, own, send = project(place, (tokens, tokens_far, grads_in, grads_far), qo, F32)
    prior_state = gate(exchange(sums_of(after(pieces, own), False)))
    recv = after(core_swap(send), prior_state)
    kv_far = core_swap(kv_near)
    queries, attn_grad, local_grad = attention_grad(
        place, own, recv, keys, after(values, kv_far), prior_state, norm_gain.reshape(1, head)
    )
    grad_pieces = exchange(local_grad)
    qo_far = core_swap(qo_near)
    base, *grads = inner_grads(
        place, queries, keys, values, attn_grad, prior_state, qo_near, qo_far
    )
    later_state = exchange(sums_of(grad_pieces, True))
    result = output(place, base, *grads, keys, values, later_state, kv_near, kv_far)
    return result[None]


def solution(mesh):
    split = Mesh(mesh.devices.reshape(mesh.shape["dp"], 4, 8, 2), DP_SEQ)
    in_specs = (P("dp", SEQ, None), P(DP_SEQ, None, None), P(DP_SEQ, None), P(), P("dp", SEQ, None))
    out_specs = P("dp", SEQ, None)
    return jax.shard_map(
        per_device, mesh=split, in_specs=in_specs, out_specs=out_specs, check_vma=False
    )
```

```python
import functools

import jax
import jax.numpy as jnp
from jax import lax
from jax.experimental import pallas as pl
from jax.experimental.pallas import tpu as pltpu
from jax.sharding import Mesh
from jax.sharding import PartitionSpec as P

SEQ = ("x", "z", "core")
DP_SEQ = ("dp", "x", "z", "core")
ROWS = ("dp", "z")
BF16 = jnp.bfloat16
F32 = jnp.float32
LIMIT = 16 * 1024 * 1024
LONG = 30_000_000_000
ANY = pl.BlockSpec(memory_space=pl.ANY)
VMEM = pl.BlockSpec(memory_space=pltpu.VMEM)


def contract(left, right, left_dim, right_dim):
    return lax.dot_general(
        left, right, (((left_dim,), (right_dim,)), ((), ())), preferred_element_type=F32
    )


def cost(flops, moved):
    return pl.CostEstimate(flops=flops, bytes_accessed=moved, transcendentals=0)


def after(value, *events):
    return lax.optimization_barrier((value, *events))[0]


def core_swap(block):
    return lax.ppermute(block, "core", [(0, 1), (1, 0)])


def in_hbm(*values):
    return [pltpu.with_memory_space_constraint(v, pltpu.HBM) for v in values]


def project_kernel(shifts, *refs):
    tokens, blocks, outs, scratch = refs[:-11], refs[-11:-7], refs[-7:-4], refs[-4:]
    weight_ref, own_ref, send_ref = outs
    own_held, far_held, own_sem, far_sem = scratch
    rows = weight_ref.shape[0] // 32
    x, core = lax.axis_index("x"), lax.axis_index("core")

    def products(own, far):
        own_copy = pltpu.make_async_copy(own, own_held, own_sem)
        far_copy = pltpu.make_async_copy(far, far_held, far_sem)
        own_copy.start()
        far_copy.start()
        for k, ref in zip(shifts, blocks):
            source = lax.rem(x - k + 4, 4)
            for p in range(8):
                at = pl.multiple_of((p * 4 + source) * rows, 64)
                weight_ref[pl.ds(at, rows), :] = ref[p * rows : (p + 1) * rows, :]
        own_copy.wait()
        own_ref[...] = contract(own_held[...], weight_ref[...], 1, 0).astype(own_ref.dtype)
        far_copy.wait()
        send_ref[...] = contract(far_held[...], weight_ref[...], 1, 0).astype(send_ref.dtype)

    if len(tokens) == 2:
        products(*tokens)
    else:
        pl.when(core == 0)(lambda: products(*tokens[:2]))
        pl.when(core != 0)(lambda: products(*tokens[2:]))


def project(tokens, blocks, dtype):
    count, depth = tokens[0].shape
    row = jax.ShapeDtypeStruct((count, 128), dtype)
    return pl.pallas_call(
        functools.partial(project_kernel, tuple(blocks)),
        out_shape=[jax.ShapeDtypeStruct((depth, 128), BF16), row, row],
        in_specs=[ANY] * len(tokens) + [VMEM] * 4,
        out_specs=[VMEM] * 3,
        scratch_shapes=[pltpu.VMEM((count, depth), BF16)] * 2 + [pltpu.SemaphoreType.DMA] * 2,
        compiler_params=pltpu.CompilerParams(vmem_limit_bytes=LIMIT),
        cost_estimate=cost(LONG, 4 * count * depth + 4 * depth * 128),
    )(*in_hbm(*tokens), *blocks.values())


def state_kernel(own_ref, recv_ref, kv_ref, state_ref):
    own, recv = own_ref[...], recv_ref[...]
    first = lax.axis_index("core") == 0
    keys, values = jnp.where(first, own, recv), jnp.where(first, recv, own)
    kv_ref[:, :128] = keys
    kv_ref[:, 128:] = values
    state_ref[...] = contract(keys, values, 0, 0).astype(BF16)


def keys_values_state(own, recv):
    return pl.pallas_call(
        state_kernel,
        out_shape=[
            jax.ShapeDtypeStruct((own.shape[0], 256), BF16),
            jax.ShapeDtypeStruct((128, 128), BF16),
        ],
        in_specs=[VMEM] * 2,
        out_specs=[VMEM] * 2,
        compiler_params=pltpu.CompilerParams(vmem_limit_bytes=LIMIT),
        cost_estimate=cost(2 * own.size * 128, 8 * own.size),
    )(own, recv)


def gate_kernel(in_ref, out_ref):
    out_ref[...] = in_ref[...]


def gate(value):
    return pl.pallas_call(
        gate_kernel,
        out_shape=jax.ShapeDtypeStruct(value.shape, value.dtype),
        in_specs=[VMEM],
        out_specs=VMEM,
        compiler_params=pltpu.CompilerParams(vmem_limit_bytes=LIMIT),
        cost_estimate=cost(LONG, 4 * value.size),
    )(value)


def causal_of(count):
    rows = lax.broadcasted_iota(jnp.int32, (count, count), 0)
    return rows >= lax.broadcasted_iota(jnp.int32, (count, count), 1)


def grad_kernel(
    near_ref, far_ref, kv_ref, prior_ref, gain_ref, qa_ref, state_ref
):
    first = lax.axis_index("core") == 0
    near, far = near_ref[...], far_ref[...]
    queries = jnp.where(first, near, far).astype(BF16)
    head_grad = jnp.where(first, far, near)
    qa_ref[:, :128] = queries
    scores = contract(queries, kv_ref[:, :128], 1, 1)
    scores = jnp.where(causal_of(scores.shape[0]), scores, 0.0).astype(BF16)
    attended = contract(scores, kv_ref[:, 128:], 1, 0) + contract(queries, prior_ref[...], 1, 0)
    inv_rms = lax.rsqrt(jnp.mean(attended * attended, axis=-1, keepdims=True) + 1e-06)
    scaled = gain_ref[...] * head_grad
    mean = jnp.mean(attended * scaled, axis=-1, keepdims=True)
    attn_grad = inv_rms * scaled - attended * (inv_rms * inv_rms * inv_rms) * mean
    attn_grad = attn_grad.astype(BF16)
    qa_ref[:, 128:] = attn_grad
    state_ref[...] = contract(queries, attn_grad, 0, 0).astype(BF16)


def attention_grad(near, far, kv, prior, gain):
    count = kv.shape[0]
    return pl.pallas_call(
        grad_kernel,
        out_shape=[
            jax.ShapeDtypeStruct((count, 256), BF16),
            jax.ShapeDtypeStruct((128, 128), BF16),
        ],
        in_specs=[VMEM] * 5,
        out_specs=[VMEM] * 2,
        compiler_params=pltpu.CompilerParams(vmem_limit_bytes=LIMIT),
        cost_estimate=cost(LONG, 16 * count * 128),
    )(near, far, kv, prior, gain)


def inner_kernel(*refs):
    rows_any, (near_any, far_any), outs, scratch = refs[:3], refs[3:5], refs[5:8], refs[8:]
    base_ref, dk_ref, dv_ref = outs
    qa_ref, kv_ref, prior_ref, weight_ref, row_sems, weight_sem = scratch

    def body(weight_any):
        weight_copy = pltpu.make_async_copy(weight_any, weight_ref, weight_sem)
        copies = [
            pltpu.make_async_copy(source, target, row_sems.at[i])
            for i, (source, target) in enumerate(zip(rows_any, scratch[:3]))
        ]
        for copy in copies:
            copy.start()
        weight_copy.start()
        for copy in copies:
            copy.wait()
        attn_grad = qa_ref[:, 128:]
        causal = causal_of(attn_grad.shape[0])
        scores = contract(qa_ref[:, :128], kv_ref[:, :128], 1, 1)
        scores = jnp.where(causal, scores, 0.0).astype(BF16)
        prob = contract(attn_grad, kv_ref[:, 128:], 1, 1)
        prob = jnp.where(causal, prob, 0.0).astype(BF16)
        query_grad = contract(prob, kv_ref[:, :128], 1, 0) + contract(attn_grad, prior_ref[...], 1, 1)
        query_grad = query_grad.astype(BF16)
        dk_ref[...] = contract(prob, qa_ref[:, :128], 0, 0)
        dv_ref[...] = contract(scores, attn_grad, 0, 0)
        weight_copy.wait()
        part = weight_ref.shape[0] // 4
        for i in range(4):
            at = slice(i * part, (i + 1) * part)
            base_ref[:, at] = contract(query_grad, weight_ref[at, :], 1, 1)

    pl.when(lax.axis_index("core") == 0)(lambda: body(near_any))
    pl.when(lax.axis_index("core") != 0)(lambda: body(far_any))


def inner_grads(qa, kv, prior, near, far):
    count, depth = kv.shape[0], near.shape[0]
    rows = pltpu.VMEM((count, 256), BF16)
    return pl.pallas_call(
        inner_kernel,
        out_shape=[
            jax.ShapeDtypeStruct((count, depth), F32),
            jax.ShapeDtypeStruct((count, 128), F32),
            jax.ShapeDtypeStruct((count, 128), F32),
        ],
        in_specs=[ANY] * 5,
        out_specs=[VMEM] * 3,
        scratch_shapes=[
            rows,
            rows,
            pltpu.VMEM((128, 128), BF16),
            pltpu.VMEM((depth, 128), BF16),
            pltpu.SemaphoreType.DMA((3,)),
            pltpu.SemaphoreType.DMA,
        ],
        compiler_params=pltpu.CompilerParams(vmem_limit_bytes=LIMIT),
        cost_estimate=cost(LONG, 4 * count * depth + 4 * depth * 128),
    )(*in_hbm(qa, kv, prior, near, far))


def output_kernel(
    base, dk, dv, kv_any, later, near_any, far_any, out_any,
    kv_ref, near_ref, far_ref, out_ref, row_sem, weight_sems, out_sems,
):
    steps, _, part = out_ref.shape
    rows = [pltpu.make_async_copy(kv_any, kv_ref, row_sem)]
    weights = []
    for i in range(steps):
        at = pl.ds(i * part, part)
        for n, (source, target) in enumerate(((near_any, near_ref), (far_any, far_ref))):
            weights.append(
                pltpu.make_async_copy(source.at[at], target.at[at], weight_sems.at[2 * i + n])
            )
    for copy in rows + weights:
        copy.start()
    for copy in rows:
        copy.wait()
    first = lax.axis_index("core") == 0
    key_grad = (dk[...] + contract(kv_ref[:, 128:], later[...], 1, 1)).astype(BF16)
    value_grad = (dv[...] + contract(kv_ref[:, :128], later[...], 1, 0)).astype(BF16)
    near_grad = jnp.where(first, key_grad, value_grad)
    far_grad = jnp.where(first, value_grad, key_grad)
    joined = jnp.concatenate([near_grad, far_grad], axis=1)
    outs = []
    for i in range(steps):
        weights[2 * i].wait()
        weights[2 * i + 1].wait()
        at = slice(i * part, (i + 1) * part)
        weight = jnp.concatenate([near_ref[at, :], far_ref[at, :]], axis=1)
        out_ref[i] = (base[:, at] + contract(joined, weight, 1, 1)).astype(BF16)
        copy = pltpu.make_async_copy(
            out_ref.at[i], out_any.at[:, pl.ds(i * part, part)], out_sems.at[i]
        )
        copy.start()
        outs.append(copy)
    for copy in outs:
        copy.wait()


def output(base, dk, dv, kv, later, near, far):
    count, depth = base.shape
    steps = 4
    return pl.pallas_call(
        output_kernel,
        out_shape=jax.ShapeDtypeStruct((count, depth), BF16),
        in_specs=[VMEM] * 3 + [ANY] + [VMEM] + [ANY] * 2,
        out_specs=ANY,
        scratch_shapes=[
            pltpu.VMEM((count, 256), BF16),
            pltpu.VMEM((depth, 128), BF16),
            pltpu.VMEM((depth, 128), BF16),
            pltpu.VMEM((steps, count, depth // steps), BF16),
            pltpu.SemaphoreType.DMA,
            pltpu.SemaphoreType.DMA((2 * steps,)),
            pltpu.SemaphoreType.DMA((steps,)),
        ],
        compiler_params=pltpu.CompilerParams(vmem_limit_bytes=LIMIT),
        cost_estimate=cost(4 * count * depth * 128, 4 * depth * 128 + 6 * count * depth),
    )(base, dk, dv, *in_hbm(kv), later, *in_hbm(near, far))


def sums_kernel(reverse, in_ref, out_ref):
    each = in_ref.shape[0] // 64
    to = lax.broadcasted_iota(jnp.int32, (128, 128), 0)
    frm = lax.broadcasted_iota(jnp.int32, (128, 128), 1)
    others = (frm // each > to // each) if reverse else (frm // each < to // each)
    mask = jnp.where(others & (frm % each == to % each), 1.0, 0.0).astype(BF16)
    out_ref[...] = contract(mask, in_ref[...], 1, 0).astype(BF16)


def sums_of(pieces, reverse):
    return pl.pallas_call(
        functools.partial(sums_kernel, reverse),
        out_shape=jax.ShapeDtypeStruct(pieces.shape, BF16),
        in_specs=[VMEM],
        out_specs=VMEM,
        compiler_params=pltpu.CompilerParams(vmem_limit_bytes=LIMIT),
        cost_estimate=cost(LONG, 4 * pieces.size),
    )(pieces)


def exchange(state):
    peers, head = lax.axis_size(SEQ), state.shape[1]
    pieces = state.reshape(peers, -1, head)
    return lax.all_to_all(pieces, SEQ, 0, 0, tiled=True).reshape(state.shape)


def per_device(inputs, w_project, w_output, norm_gain, out_grad):
    tokens = inputs[0]
    grads_in = out_grad[0]
    head = w_output.shape[1]
    dps, zs, xs = lax.axis_size("dp"), lax.axis_size("z"), lax.axis_size("x")
    on_first = lax.axis_index("core") == 0

    rows = jnp.concatenate([w_project.reshape(-1, 3 * head), w_output], axis=1)
    rows = lax.all_gather(rows, "core", axis=0, tiled=True)
    kv_rows = jnp.where(on_first, rows[:, head : 2 * head], rows[:, 2 * head : 3 * head])
    qo_rows = jnp.where(on_first, rows[:, :head], rows[:, 3 * head :])

    def copied(block):
        return jnp.broadcast_to(block[None], (dps * zs, *block.shape))

    def over_planes(copies):
        return lax.all_to_all(copies, ROWS, 0, 0, tiled=True).reshape(-1, head)

    def over_x(block):
        shifts = {k: lax.ppermute(block, "x", [(i, (i + k) % xs) for i in range(xs)]) for k in (2, 1, 3)}
        return {1: shifts[1], 3: shifts[3], 2: shifts[2], 0: block}

    kv_copies = copied(kv_rows)
    tokens_far = core_swap(after(tokens, kv_copies))
    grads_far = core_swap(after(grads_in, kv_copies))
    kv_plane = over_planes(kv_copies)
    qo_plane = over_planes(copied(gate(after(qo_rows, kv_plane))))
    tokens_far = after(tokens_far, grads_far)
    kv_near, own, send = project((tokens, tokens_far), over_x(kv_plane), BF16)
    own, qo_plane = lax.optimization_barrier((own, qo_plane))
    kv, local_state = keys_values_state(own, core_swap(send))

    qo = over_x(after(qo_plane, local_state))
    prior_state = gate(exchange(sums_of(exchange(local_state), False)))
    qo_near, own, send = project(
        (tokens, tokens_far, grads_in, grads_far), qo, F32
    )
    recv = after(core_swap(send), prior_state)
    qa, local_grad = attention_grad(own, recv, kv, prior_state, norm_gain.reshape(1, head))
    kv_far = core_swap(kv_near)
    grad_pieces = exchange(local_grad)
    qo_far = core_swap(qo_near)
    base, *grads = inner_grads(qa, kv, prior_state, qo_near, qo_far)
    later_state = exchange(sums_of(grad_pieces, True))
    result = output(base, *grads, kv, later_state, kv_near, kv_far)
    return result[None]


def solution(mesh):
    split = Mesh(mesh.devices.reshape(mesh.shape["dp"], 4, 8, 2), DP_SEQ)
    in_specs = (P("dp", SEQ, None), P(DP_SEQ, None, None), P(DP_SEQ, None), P(), P("dp", SEQ, None))
    out_specs = P("dp", SEQ, None)
    return jax.shard_map(
        per_device, mesh=split, in_specs=in_specs, out_specs=out_specs, check_vma=False
    )
```

```python
import functools

import jax
import jax.numpy as jnp
from jax import lax
from jax.experimental import pallas as pl
from jax.experimental.pallas import tpu as pltpu
from jax.sharding import Mesh
from jax.sharding import PartitionSpec as P

SEQ = ("x", "z", "core")
DP_SEQ = ("dp", "x", "z", "core")
ROWS = ("dp", "z")
BF16 = jnp.bfloat16
F32 = jnp.float32
LIMIT = 16 * 1024 * 1024
LONG = 80_000_000_000
ANY = pl.BlockSpec(memory_space=pl.ANY)
VMEM = pl.BlockSpec(memory_space=pltpu.VMEM)


def contract(left, right, left_dim, right_dim):
    return lax.dot_general(
        left, right, (((left_dim,), (right_dim,)), ((), ())), preferred_element_type=F32
    )


def cost(flops, moved):
    return pl.CostEstimate(flops=flops, bytes_accessed=moved, transcendentals=0)


def after(value, *events):
    return lax.optimization_barrier((value, *events))[0]


def core_swap(block):
    return lax.ppermute(block, "core", [(0, 1), (1, 0)])


def in_hbm(*values):
    return [pltpu.with_memory_space_constraint(v, pltpu.HBM) for v in values]


def project_kernel(shifts, slot, *refs):
    given, outs, scratch = refs[:-9], refs[-9:-6], refs[-6:]
    tokens, blocks = given[: 2 + 2 * slot], given[2 + 2 * slot : 6 + 2 * slot]
    weights_any, own_ref, send_ref = outs
    own_held, far_held, weight_ref, own_sem, far_sem, weight_sem = scratch
    rows = weight_ref.shape[0] // 32
    x, core = lax.axis_index("x"), lax.axis_index("core")

    def products(own, far):
        own_copy = pltpu.make_async_copy(own, own_held, own_sem)
        far_copy = pltpu.make_async_copy(far, far_held, far_sem)
        own_copy.start()
        far_copy.start()
        for k, ref in zip(shifts, blocks):
            source = lax.rem(x - k + 4, 4)
            for p in range(8):
                at = pl.multiple_of((p * 4 + source) * rows, 64)
                weight_ref[pl.ds(at, rows), :] = ref[p * rows : (p + 1) * rows, :]
        weight_copy = pltpu.make_async_copy(weight_ref, weights_any.at[slot], weight_sem)
        weight_copy.start()
        own_copy.wait()
        own_ref[...] = contract(own_held[...], weight_ref[...], 1, 0).astype(own_ref.dtype)
        far_copy.wait()
        send_ref[...] = contract(far_held[...], weight_ref[...], 1, 0).astype(send_ref.dtype)
        weight_copy.wait()

    if len(tokens) == 2:
        products(*tokens)
    else:
        pl.when(core == 0)(lambda: products(*tokens[:2]))
        pl.when(core != 0)(lambda: products(*tokens[2:]))


def project(tokens, blocks, dtype, *held):
    count, depth = tokens[0].shape
    slot = len(held)
    row = jax.ShapeDtypeStruct((count, 128), dtype)
    return pl.pallas_call(
        functools.partial(project_kernel, tuple(blocks), slot),
        out_shape=[pltpu.HBM((2, depth, 128), BF16), row, row],
        in_specs=[ANY] * len(tokens) + [VMEM] * 4 + [ANY] * slot,
        out_specs=[ANY, VMEM, VMEM],
        input_output_aliases={len(tokens) + 4: 0} if held else {},
        scratch_shapes=[
            pltpu.VMEM((count, depth), BF16),
            pltpu.VMEM((count, depth), BF16),
            pltpu.VMEM((depth, 128), BF16),
            *[pltpu.SemaphoreType.DMA] * 3,
        ],
        compiler_params=pltpu.CompilerParams(vmem_limit_bytes=LIMIT),
        cost_estimate=cost(LONG, 4 * count * depth + 4 * depth * 128),
    )(*in_hbm(*tokens), *blocks.values(), *in_hbm(*held))


def state_kernel(own_ref, recv_ref, kv_ref, state_ref):
    own, recv = own_ref[...], recv_ref[...]
    first = lax.axis_index("core") == 0
    keys, values = jnp.where(first, own, recv), jnp.where(first, recv, own)
    kv_ref[:, :128] = keys
    kv_ref[:, 128:] = values
    state_ref[...] = contract(keys, values, 0, 0).astype(BF16)


def keys_values_state(own, recv):
    return pl.pallas_call(
        state_kernel,
        out_shape=[
            jax.ShapeDtypeStruct((own.shape[0], 256), BF16),
            jax.ShapeDtypeStruct((128, 128), BF16),
        ],
        in_specs=[VMEM] * 2,
        out_specs=[VMEM] * 2,
        compiler_params=pltpu.CompilerParams(vmem_limit_bytes=LIMIT),
        cost_estimate=cost(2 * own.size * 128, 8 * own.size),
    )(own, recv)


def gate_kernel(in_ref, out_ref):
    out_ref[...] = in_ref[...]


def gate(value):
    return pl.pallas_call(
        gate_kernel,
        out_shape=jax.ShapeDtypeStruct(value.shape, value.dtype),
        in_specs=[VMEM],
        out_specs=VMEM,
        compiler_params=pltpu.CompilerParams(vmem_limit_bytes=LIMIT),
        cost_estimate=cost(LONG, 4 * value.size),
    )(value)


def copies_kernel(in_ref, out_ref):
    out_ref[...] = jnp.broadcast_to(in_ref[...][None], out_ref.shape)


def gated_copies(block, peers):
    return pl.pallas_call(
        copies_kernel,
        out_shape=jax.ShapeDtypeStruct((peers, *block.shape), block.dtype),
        in_specs=[VMEM],
        out_specs=VMEM,
        compiler_params=pltpu.CompilerParams(vmem_limit_bytes=LIMIT),
        cost_estimate=cost(LONG, 2 * peers * block.size),
    )(block)


def causal_of(count):
    rows = lax.broadcasted_iota(jnp.int32, (count, count), 0)
    return rows >= lax.broadcasted_iota(jnp.int32, (count, count), 1)


def grad_kernel(
    near_ref, far_ref, kv_ref, prior_ref, gain_ref, qa_ref, state_ref
):
    first = lax.axis_index("core") == 0
    near, far = near_ref[...], far_ref[...]
    queries = jnp.where(first, near, far).astype(BF16)
    head_grad = jnp.where(first, far, near)
    qa_ref[:, :128] = queries
    scores = contract(queries, kv_ref[:, :128], 1, 1)
    scores = jnp.where(causal_of(scores.shape[0]), scores, 0.0).astype(BF16)
    attended = contract(scores, kv_ref[:, 128:], 1, 0) + contract(queries, prior_ref[...], 1, 0)
    inv_rms = lax.rsqrt(jnp.mean(attended * attended, axis=-1, keepdims=True) + 1e-06)
    scaled = gain_ref[...] * head_grad
    mean = jnp.mean(attended * scaled, axis=-1, keepdims=True)
    attn_grad = inv_rms * scaled - attended * (inv_rms * inv_rms * inv_rms) * mean
    attn_grad = attn_grad.astype(BF16)
    qa_ref[:, 128:] = attn_grad
    state_ref[...] = contract(queries, attn_grad, 0, 0).astype(BF16)


def attention_grad(near, far, kv, prior, gain):
    count = kv.shape[0]
    return pl.pallas_call(
        grad_kernel,
        out_shape=[
            jax.ShapeDtypeStruct((count, 256), BF16),
            jax.ShapeDtypeStruct((128, 128), BF16),
        ],
        in_specs=[VMEM] * 5,
        out_specs=[VMEM] * 2,
        compiler_params=pltpu.CompilerParams(vmem_limit_bytes=LIMIT),
        cost_estimate=cost(LONG, 16 * count * 128),
    )(near, far, kv, prior, gain)


def inner_kernel(*refs):
    rows_any, (near_any, far_any), outs, scratch = refs[:3], refs[3:5], refs[5:8], refs[8:]
    base_ref, dk_ref, dv_ref = outs
    qa_ref, kv_ref, prior_ref, weight_ref, row_sems, weight_sem = scratch

    def body(weight_any):
        weight_copy = pltpu.make_async_copy(weight_any.at[1], weight_ref, weight_sem)
        copies = [
            pltpu.make_async_copy(source, target, row_sems.at[i])
            for i, (source, target) in enumerate(zip(rows_any, scratch[:3]))
        ]
        for copy in copies:
            copy.start()
        weight_copy.start()
        for copy in copies:
            copy.wait()
        attn_grad = qa_ref[:, 128:]
        causal = causal_of(attn_grad.shape[0])
        scores = contract(qa_ref[:, :128], kv_ref[:, :128], 1, 1)
        scores = jnp.where(causal, scores, 0.0).astype(BF16)
        prob = contract(attn_grad, kv_ref[:, 128:], 1, 1)
        prob = jnp.where(causal, prob, 0.0).astype(BF16)
        query_grad = contract(prob, kv_ref[:, :128], 1, 0) + contract(attn_grad, prior_ref[...], 1, 1)
        query_grad = query_grad.astype(BF16)
        dk_ref[...] = contract(prob, qa_ref[:, :128], 0, 0)
        dv_ref[...] = contract(scores, attn_grad, 0, 0)
        weight_copy.wait()
        part = weight_ref.shape[0] // 4
        for i in range(4):
            at = slice(i * part, (i + 1) * part)
            base_ref[:, at] = contract(query_grad, weight_ref[at, :], 1, 1)

    pl.when(lax.axis_index("core") == 0)(lambda: body(near_any))
    pl.when(lax.axis_index("core") != 0)(lambda: body(far_any))


def inner_grads(qa, kv, prior, near, far):
    count, depth = kv.shape[0], near.shape[1]
    rows = pltpu.VMEM((count, 256), BF16)
    return pl.pallas_call(
        inner_kernel,
        out_shape=[
            jax.ShapeDtypeStruct((count, depth), F32),
            jax.ShapeDtypeStruct((count, 128), F32),
            jax.ShapeDtypeStruct((count, 128), F32),
        ],
        in_specs=[ANY] * 5,
        out_specs=[VMEM] * 3,
        scratch_shapes=[
            rows,
            rows,
            pltpu.VMEM((128, 128), BF16),
            pltpu.VMEM((depth, 128), BF16),
            pltpu.SemaphoreType.DMA((3,)),
            pltpu.SemaphoreType.DMA,
        ],
        compiler_params=pltpu.CompilerParams(vmem_limit_bytes=LIMIT),
        cost_estimate=cost(LONG, 4 * count * depth + 4 * depth * 128),
    )(*in_hbm(qa, kv, prior, near, far))


def output_kernel(
    base, dk, dv, kv_any, later, near_any, far_any, out_any,
    kv_ref, near_ref, far_ref, out_ref, row_sem, weight_sems, out_sems,
):
    steps, _, part = out_ref.shape
    rows = [pltpu.make_async_copy(kv_any, kv_ref, row_sem)]
    weights = []
    for i in range(steps):
        at = pl.ds(i * part, part)
        for n, (source, target) in enumerate(((near_any, near_ref), (far_any, far_ref))):
            weights.append(
                pltpu.make_async_copy(source.at[0, at], target.at[at], weight_sems.at[2 * i + n])
            )
    for copy in rows + weights:
        copy.start()
    for copy in rows:
        copy.wait()
    first = lax.axis_index("core") == 0
    key_grad = (dk[...] + contract(kv_ref[:, 128:], later[...], 1, 1)).astype(BF16)
    value_grad = (dv[...] + contract(kv_ref[:, :128], later[...], 1, 0)).astype(BF16)
    near_grad = jnp.where(first, key_grad, value_grad)
    far_grad = jnp.where(first, value_grad, key_grad)
    joined = jnp.concatenate([near_grad, far_grad], axis=1)
    outs = []
    for i in range(steps):
        weights[2 * i].wait()
        weights[2 * i + 1].wait()
        at = slice(i * part, (i + 1) * part)
        weight = jnp.concatenate([near_ref[at, :], far_ref[at, :]], axis=1)
        out_ref[i] = (base[:, at] + contract(joined, weight, 1, 1)).astype(BF16)
        copy = pltpu.make_async_copy(
            out_ref.at[i], out_any.at[:, pl.ds(i * part, part)], out_sems.at[i]
        )
        copy.start()
        outs.append(copy)
    for copy in outs:
        copy.wait()


def output(base, dk, dv, kv, later, near, far):
    count, depth = base.shape
    steps = 4
    return pl.pallas_call(
        output_kernel,
        out_shape=jax.ShapeDtypeStruct((count, depth), BF16),
        in_specs=[VMEM] * 3 + [ANY] + [VMEM] + [ANY] * 2,
        out_specs=ANY,
        scratch_shapes=[
            pltpu.VMEM((count, 256), BF16),
            pltpu.VMEM((depth, 128), BF16),
            pltpu.VMEM((depth, 128), BF16),
            pltpu.VMEM((steps, count, depth // steps), BF16),
            pltpu.SemaphoreType.DMA,
            pltpu.SemaphoreType.DMA((2 * steps,)),
            pltpu.SemaphoreType.DMA((steps,)),
        ],
        compiler_params=pltpu.CompilerParams(vmem_limit_bytes=LIMIT),
        cost_estimate=cost(4 * count * depth * 128, 4 * depth * 128 + 6 * count * depth),
    )(base, dk, dv, *in_hbm(kv), later, *in_hbm(near, far))


def sums_kernel(reverse, in_ref, out_ref):
    each = in_ref.shape[0] // 64
    to = lax.broadcasted_iota(jnp.int32, (128, 128), 0)
    frm = lax.broadcasted_iota(jnp.int32, (128, 128), 1)
    others = (frm // each > to // each) if reverse else (frm // each < to // each)
    mask = jnp.where(others & (frm % each == to % each), 1.0, 0.0).astype(BF16)
    out_ref[...] = contract(mask, in_ref[...], 1, 0).astype(BF16)


def sums_of(pieces, reverse):
    return pl.pallas_call(
        functools.partial(sums_kernel, reverse),
        out_shape=jax.ShapeDtypeStruct(pieces.shape, BF16),
        in_specs=[VMEM],
        out_specs=VMEM,
        compiler_params=pltpu.CompilerParams(vmem_limit_bytes=LIMIT),
        cost_estimate=cost(LONG, 4 * pieces.size),
    )(pieces)


def exchange(state):
    peers, head = lax.axis_size(SEQ), state.shape[1]
    pieces = state.reshape(peers, -1, head)
    return lax.all_to_all(pieces, SEQ, 0, 0, tiled=True).reshape(state.shape)


def per_device(inputs, w_project, w_output, norm_gain, out_grad):
    tokens = inputs[0]
    grads_in = out_grad[0]
    head = w_output.shape[1]
    dps, zs, xs = lax.axis_size("dp"), lax.axis_size("z"), lax.axis_size("x")
    on_first = lax.axis_index("core") == 0

    rows = jnp.concatenate([w_project.reshape(-1, 3 * head), w_output], axis=1)
    rows = lax.all_gather(rows, "core", axis=0, tiled=True)
    kv_rows = jnp.where(on_first, rows[:, head : 2 * head], rows[:, 2 * head : 3 * head])
    qo_rows = jnp.where(on_first, rows[:, :head], rows[:, 3 * head :])

    def copied(block):
        return jnp.broadcast_to(block[None], (dps * zs, *block.shape))

    def over_planes(copies):
        return lax.all_to_all(copies, ROWS, 0, 0, tiled=True).reshape(-1, head)

    def over_x(block):
        shifts = {k: lax.ppermute(block, "x", [(i, (i + k) % xs) for i in range(xs)]) for k in (2, 1, 3)}
        return {1: shifts[1], 3: shifts[3], 2: shifts[2], 0: block}

    kv_copies = copied(kv_rows)
    tokens_far = core_swap(after(tokens, kv_copies))
    grads_far = core_swap(after(grads_in, kv_copies))
    kv_plane = over_planes(kv_copies)
    qo_plane = over_planes(gated_copies(after(qo_rows, kv_plane), dps * zs))
    tokens_far = after(tokens_far, grads_far)
    weights, own, send = project((tokens, tokens_far), over_x(kv_plane), BF16)
    own, qo_plane = lax.optimization_barrier((own, qo_plane))
    kv, local_state = keys_values_state(own, core_swap(send))

    qo = over_x(after(qo_plane, local_state))
    prior_state = gate(exchange(sums_of(exchange(local_state), False)))
    weights, own, send = project(
        (tokens, tokens_far, grads_in, grads_far), qo, F32, weights
    )
    recv = after(core_swap(send), prior_state)
    qa, local_grad = attention_grad(own, recv, kv, prior_state, norm_gain.reshape(1, head))
    grad_pieces = exchange(local_grad)
    weights_far = core_swap(weights)
    base, *grads = inner_grads(qa, kv, prior_state, weights, weights_far)
    later_state = exchange(sums_of(grad_pieces, True))
    result = output(base, *grads, kv, later_state, weights, weights_far)
    return result[None]


def solution(mesh):
    split = Mesh(mesh.devices.reshape(mesh.shape["dp"], 4, 8, 2), DP_SEQ)
    in_specs = (P("dp", SEQ, None), P(DP_SEQ, None, None), P(DP_SEQ, None), P(), P("dp", SEQ, None))
    out_specs = P("dp", SEQ, None)
    return jax.shard_map(
        per_device, mesh=split, in_specs=in_specs, out_specs=out_specs, check_vma=False
    )
```

```python
import functools

import jax
import jax.numpy as jnp
from jax import lax
from jax.experimental import pallas as pl
from jax.experimental.pallas import tpu as pltpu
from jax.sharding import Mesh
from jax.sharding import PartitionSpec as P

SEQ = ("x", "z", "core")
DP_SEQ = ("dp", "x", "z", "core")
ROWS = ("dp", "z")
BF16 = jnp.bfloat16
F32 = jnp.float32
LIMIT = 16 * 1024 * 1024
LONG = 80_000_000_000
ANY = pl.BlockSpec(memory_space=pl.ANY)
VMEM = pl.BlockSpec(memory_space=pltpu.VMEM)


def contract(left, right, left_dim, right_dim):
    return lax.dot_general(
        left, right, (((left_dim,), (right_dim,)), ((), ())), preferred_element_type=F32
    )


def cost(flops, moved):
    return pl.CostEstimate(flops=flops, bytes_accessed=moved, transcendentals=0)


def after(value, *events):
    return lax.optimization_barrier((value, *events))[0]


def core_swap(block):
    return lax.ppermute(block, "core", [(0, 1), (1, 0)])


def in_hbm(*values):
    return [pltpu.with_memory_space_constraint(v, pltpu.HBM) for v in values]


def project_kernel(shifts, slot, *refs):
    given, outs, scratch = refs[:-9], refs[-9:-6], refs[-6:]
    tokens, blocks = given[: 2 + 2 * slot], given[2 + 2 * slot : 6 + 2 * slot]
    weights_any, own_ref, send_ref = outs
    own_held, far_held, weight_ref, own_sem, far_sem, weight_sem = scratch
    rows = weight_ref.shape[0] // 32
    x, core = lax.axis_index("x"), lax.axis_index("core")

    def products(own, far):
        own_copy = pltpu.make_async_copy(own, own_held, own_sem)
        far_copy = pltpu.make_async_copy(far, far_held, far_sem)
        own_copy.start()
        far_copy.start()
        for k, ref in zip(shifts, blocks):
            source = lax.rem(x - k + 4, 4)
            for p in range(8):
                at = pl.multiple_of((p * 4 + source) * rows, 64)
                weight_ref[pl.ds(at, rows), :] = ref[p * rows : (p + 1) * rows, :]
        weight_copy = pltpu.make_async_copy(weight_ref, weights_any.at[slot], weight_sem)
        weight_copy.start()
        own_copy.wait()
        own_ref[...] = contract(own_held[...], weight_ref[...], 1, 0).astype(own_ref.dtype)
        far_copy.wait()
        send_ref[...] = contract(far_held[...], weight_ref[...], 1, 0).astype(send_ref.dtype)
        weight_copy.wait()

    if len(tokens) == 2:
        products(*tokens)
    else:
        pl.when(core == 0)(lambda: products(*tokens[:2]))
        pl.when(core != 0)(lambda: products(*tokens[2:]))


def project(tokens, blocks, dtype, *held):
    count, depth = tokens[0].shape
    slot = len(held)
    row = jax.ShapeDtypeStruct((count, 128), dtype)
    return pl.pallas_call(
        functools.partial(project_kernel, tuple(blocks), slot),
        out_shape=[pltpu.HBM((2, depth, 128), BF16), row, row],
        in_specs=[ANY] * len(tokens) + [VMEM] * 4 + [ANY] * slot,
        out_specs=[ANY, VMEM, VMEM],
        input_output_aliases={len(tokens) + 4: 0} if held else {},
        scratch_shapes=[
            pltpu.VMEM((count, depth), BF16),
            pltpu.VMEM((count, depth), BF16),
            pltpu.VMEM((depth, 128), BF16),
            *[pltpu.SemaphoreType.DMA] * 3,
        ],
        compiler_params=pltpu.CompilerParams(vmem_limit_bytes=LIMIT),
        cost_estimate=cost(LONG, 4 * count * depth + 4 * depth * 128),
    )(*in_hbm(*tokens), *blocks.values(), *in_hbm(*held))


def state_kernel(own_ref, recv_ref, kv_ref, state_ref):
    own, recv = own_ref[...], recv_ref[...]
    first = lax.axis_index("core") == 0
    keys, values = jnp.where(first, own, recv), jnp.where(first, recv, own)
    kv_ref[:, :128] = keys
    kv_ref[:, 128:] = values
    state_ref[...] = contract(keys, values, 0, 0).astype(BF16)


def keys_values_state(own, recv):
    return pl.pallas_call(
        state_kernel,
        out_shape=[
            jax.ShapeDtypeStruct((own.shape[0], 256), BF16),
            jax.ShapeDtypeStruct((128, 128), BF16),
        ],
        in_specs=[VMEM] * 2,
        out_specs=[VMEM] * 2,
        compiler_params=pltpu.CompilerParams(vmem_limit_bytes=LIMIT),
        cost_estimate=cost(2 * own.size * 128, 8 * own.size),
    )(own, recv)


def gate_kernel(in_ref, out_ref):
    out_ref[...] = in_ref[...]


def gate(value):
    return pl.pallas_call(
        gate_kernel,
        out_shape=jax.ShapeDtypeStruct(value.shape, value.dtype),
        in_specs=[VMEM],
        out_specs=VMEM,
        compiler_params=pltpu.CompilerParams(vmem_limit_bytes=LIMIT),
        cost_estimate=cost(LONG, 4 * value.size),
    )(value)


def copies_kernel(in_ref, out_ref):
    out_ref[...] = jnp.broadcast_to(in_ref[...][None], out_ref.shape)


def gated_copies(block, peers):
    return pl.pallas_call(
        copies_kernel,
        out_shape=jax.ShapeDtypeStruct((peers, *block.shape), block.dtype),
        in_specs=[VMEM],
        out_specs=VMEM,
        compiler_params=pltpu.CompilerParams(vmem_limit_bytes=LIMIT),
        cost_estimate=cost(LONG, 2 * peers * block.size),
    )(block)


def causal_of(count):
    rows = lax.broadcasted_iota(jnp.int32, (count, count), 0)
    return rows >= lax.broadcasted_iota(jnp.int32, (count, count), 1)


def grad_kernel(
    near_ref, far_ref, kv_ref, prior_ref, gain_ref, qa_any, state_ref, qa_ref, qa_sem
):
    first = lax.axis_index("core") == 0
    near, far = near_ref[...], far_ref[...]
    queries = jnp.where(first, near, far).astype(BF16)
    head_grad = jnp.where(first, far, near)
    qa_ref[:, :128] = queries
    scores = contract(queries, kv_ref[:, :128], 1, 1)
    scores = jnp.where(causal_of(scores.shape[0]), scores, 0.0).astype(BF16)
    attended = contract(scores, kv_ref[:, 128:], 1, 0) + contract(queries, prior_ref[...], 1, 0)
    inv_rms = lax.rsqrt(jnp.mean(attended * attended, axis=-1, keepdims=True) + 1e-06)
    scaled = gain_ref[...] * head_grad
    mean = jnp.mean(attended * scaled, axis=-1, keepdims=True)
    attn_grad = inv_rms * scaled - attended * (inv_rms * inv_rms * inv_rms) * mean
    attn_grad = attn_grad.astype(BF16)
    qa_ref[:, 128:] = attn_grad
    copy = pltpu.make_async_copy(qa_ref, qa_any, qa_sem)
    copy.start()
    state_ref[...] = contract(queries, attn_grad, 0, 0).astype(BF16)
    copy.wait()


def attention_grad(near, far, kv, prior, gain):
    count = kv.shape[0]
    return pl.pallas_call(
        grad_kernel,
        out_shape=[
            pltpu.HBM((count, 256), BF16),
            jax.ShapeDtypeStruct((128, 128), BF16),
        ],
        in_specs=[VMEM] * 5,
        out_specs=[ANY, VMEM],
        scratch_shapes=[pltpu.VMEM((count, 256), BF16), pltpu.SemaphoreType.DMA],
        compiler_params=pltpu.CompilerParams(vmem_limit_bytes=LIMIT),
        cost_estimate=cost(LONG, 16 * count * 128),
    )(near, far, kv, prior, gain)


def inner_kernel(*refs):
    rows_any, (near_any, far_any), outs, scratch = refs[:3], refs[3:5], refs[5:8], refs[8:]
    base_ref, dk_ref, dv_ref = outs
    qa_ref, kv_ref, prior_ref, weight_ref, row_sems, weight_sem = scratch

    def body(weight_any):
        weight_copy = pltpu.make_async_copy(weight_any.at[1], weight_ref, weight_sem)
        copies = [
            pltpu.make_async_copy(source, target, row_sems.at[i])
            for i, (source, target) in enumerate(zip(rows_any, scratch[:3]))
        ]
        for copy in copies:
            copy.start()
        weight_copy.start()
        for copy in copies:
            copy.wait()
        attn_grad = qa_ref[:, 128:]
        causal = causal_of(attn_grad.shape[0])
        scores = contract(qa_ref[:, :128], kv_ref[:, :128], 1, 1)
        scores = jnp.where(causal, scores, 0.0).astype(BF16)
        prob = contract(attn_grad, kv_ref[:, 128:], 1, 1)
        prob = jnp.where(causal, prob, 0.0).astype(BF16)
        query_grad = contract(prob, kv_ref[:, :128], 1, 0) + contract(attn_grad, prior_ref[...], 1, 1)
        query_grad = query_grad.astype(BF16)
        dk_ref[...] = contract(prob, qa_ref[:, :128], 0, 0)
        dv_ref[...] = contract(scores, attn_grad, 0, 0)
        weight_copy.wait()
        part = weight_ref.shape[0] // 4
        for i in range(4):
            at = slice(i * part, (i + 1) * part)
            base_ref[:, at] = contract(query_grad, weight_ref[at, :], 1, 1)

    pl.when(lax.axis_index("core") == 0)(lambda: body(near_any))
    pl.when(lax.axis_index("core") != 0)(lambda: body(far_any))


def inner_grads(qa, kv, prior, near, far):
    count, depth = kv.shape[0], near.shape[1]
    rows = pltpu.VMEM((count, 256), BF16)
    return pl.pallas_call(
        inner_kernel,
        out_shape=[
            jax.ShapeDtypeStruct((count, depth), F32),
            jax.ShapeDtypeStruct((count, 128), F32),
            jax.ShapeDtypeStruct((count, 128), F32),
        ],
        in_specs=[ANY] * 5,
        out_specs=[VMEM] * 3,
        scratch_shapes=[
            rows,
            rows,
            pltpu.VMEM((128, 128), BF16),
            pltpu.VMEM((depth, 128), BF16),
            pltpu.SemaphoreType.DMA((3,)),
            pltpu.SemaphoreType.DMA,
        ],
        compiler_params=pltpu.CompilerParams(vmem_limit_bytes=LIMIT),
        cost_estimate=cost(LONG, 4 * count * depth + 4 * depth * 128),
    )(*in_hbm(qa, kv, prior, near, far))


def output_kernel(
    base, dk, dv, kv_any, later, near_any, far_any, out_any,
    kv_ref, near_ref, far_ref, out_ref, row_sem, weight_sems, out_sems,
):
    steps, _, part = out_ref.shape
    rows = [pltpu.make_async_copy(kv_any, kv_ref, row_sem)]
    weights = []
    for i in range(steps):
        at = pl.ds(i * part, part)
        for n, (source, target) in enumerate(((near_any, near_ref), (far_any, far_ref))):
            weights.append(
                pltpu.make_async_copy(source.at[0, at], target.at[at], weight_sems.at[2 * i + n])
            )
    for copy in rows + weights:
        copy.start()
    for copy in rows:
        copy.wait()
    first = lax.axis_index("core") == 0
    key_grad = (dk[...] + contract(kv_ref[:, 128:], later[...], 1, 1)).astype(BF16)
    value_grad = (dv[...] + contract(kv_ref[:, :128], later[...], 1, 0)).astype(BF16)
    near_grad = jnp.where(first, key_grad, value_grad)
    far_grad = jnp.where(first, value_grad, key_grad)
    joined = jnp.concatenate([near_grad, far_grad], axis=1)
    outs = []
    for i in range(steps):
        weights[2 * i].wait()
        weights[2 * i + 1].wait()
        at = slice(i * part, (i + 1) * part)
        weight = jnp.concatenate([near_ref[at, :], far_ref[at, :]], axis=1)
        out_ref[i] = (base[:, at] + contract(joined, weight, 1, 1)).astype(BF16)
        copy = pltpu.make_async_copy(
            out_ref.at[i], out_any.at[:, pl.ds(i * part, part)], out_sems.at[i]
        )
        copy.start()
        outs.append(copy)
    for copy in outs:
        copy.wait()


def output(base, dk, dv, kv, later, near, far):
    count, depth = base.shape
    steps = 2
    return pl.pallas_call(
        output_kernel,
        out_shape=jax.ShapeDtypeStruct((count, depth), BF16),
        in_specs=[VMEM] * 3 + [ANY] + [VMEM] + [ANY] * 2,
        out_specs=ANY,
        scratch_shapes=[
            pltpu.VMEM((count, 256), BF16),
            pltpu.VMEM((depth, 128), BF16),
            pltpu.VMEM((depth, 128), BF16),
            pltpu.VMEM((steps, count, depth // steps), BF16),
            pltpu.SemaphoreType.DMA,
            pltpu.SemaphoreType.DMA((2 * steps,)),
            pltpu.SemaphoreType.DMA((steps,)),
        ],
        compiler_params=pltpu.CompilerParams(vmem_limit_bytes=LIMIT),
        cost_estimate=cost(4 * count * depth * 128, 4 * depth * 128 + 6 * count * depth),
    )(base, dk, dv, *in_hbm(kv), later, *in_hbm(near, far))


def sums_kernel(reverse, in_ref, out_ref):
    each = in_ref.shape[0] // 64
    to = lax.broadcasted_iota(jnp.int32, (128, 128), 0)
    frm = lax.broadcasted_iota(jnp.int32, (128, 128), 1)
    others = (frm // each > to // each) if reverse else (frm // each < to // each)
    mask = jnp.where(others & (frm % each == to % each), 1.0, 0.0).astype(BF16)
    out_ref[...] = contract(mask, in_ref[...], 1, 0).astype(BF16)


def sums_of(pieces, reverse):
    return pl.pallas_call(
        functools.partial(sums_kernel, reverse),
        out_shape=jax.ShapeDtypeStruct(pieces.shape, BF16),
        in_specs=[VMEM],
        out_specs=VMEM,
        compiler_params=pltpu.CompilerParams(vmem_limit_bytes=LIMIT),
        cost_estimate=cost(LONG, 4 * pieces.size),
    )(pieces)


def exchange(state):
    peers, head = lax.axis_size(SEQ), state.shape[1]
    pieces = state.reshape(peers, -1, head)
    return lax.all_to_all(pieces, SEQ, 0, 0, tiled=True).reshape(state.shape)


def per_device(inputs, w_project, w_output, norm_gain, out_grad):
    tokens = inputs[0]
    grads_in = out_grad[0]
    head = w_output.shape[1]
    dps, zs, xs = lax.axis_size("dp"), lax.axis_size("z"), lax.axis_size("x")
    on_first = lax.axis_index("core") == 0

    rows = jnp.concatenate([w_project.reshape(-1, 3 * head), w_output], axis=1)
    rows = lax.all_gather(rows, "core", axis=0, tiled=True)
    kv_rows = jnp.where(on_first, rows[:, head : 2 * head], rows[:, 2 * head : 3 * head])
    qo_rows = jnp.where(on_first, rows[:, :head], rows[:, 3 * head :])

    def copied(block):
        return jnp.broadcast_to(block[None], (dps * zs, *block.shape))

    def over_planes(copies):
        return lax.all_to_all(copies, ROWS, 0, 0, tiled=True).reshape(-1, head)

    def over_x(block):
        shifts = {k: lax.ppermute(block, "x", [(i, (i + k) % xs) for i in range(xs)]) for k in (2, 1, 3)}
        return {1: shifts[1], 3: shifts[3], 2: shifts[2], 0: block}

    kv_copies = copied(kv_rows)
    tokens_far = core_swap(after(tokens, kv_copies))
    grads_far = core_swap(after(grads_in, kv_copies))
    kv_plane = over_planes(kv_copies)
    qo_plane = over_planes(gated_copies(after(qo_rows, kv_plane), dps * zs))
    tokens_far = after(tokens_far, grads_far)
    weights, own, send = project((tokens, tokens_far), over_x(kv_plane), BF16)
    own, qo_plane = lax.optimization_barrier((own, qo_plane))
    kv, local_state = keys_values_state(own, core_swap(send))

    qo = over_x(after(qo_plane, local_state))
    prior_state = gate(exchange(sums_of(exchange(local_state), False)))
    weights, own, send = project(
        (tokens, tokens_far, grads_in, grads_far), qo, F32, weights
    )
    recv = after(core_swap(send), prior_state)
    qa, local_grad = attention_grad(own, recv, kv, prior_state, norm_gain.reshape(1, head))
    grad_pieces = exchange(local_grad)
    weights_far = core_swap(weights)
    base, *grads = inner_grads(qa, kv, prior_state, weights, weights_far)
    later_state = exchange(sums_of(grad_pieces, True))
    result = output(base, *grads, kv, later_state, weights, weights_far)
    return result[None]


def solution(mesh):
    split = Mesh(mesh.devices.reshape(mesh.shape["dp"], 4, 8, 2), DP_SEQ)
    in_specs = (P("dp", SEQ, None), P(DP_SEQ, None, None), P(DP_SEQ, None), P(), P("dp", SEQ, None))
    out_specs = P("dp", SEQ, None)
    return jax.shard_map(
        per_device, mesh=split, in_specs=in_specs, out_specs=out_specs, check_vma=False
    )
```
